32 devices in a mesh: tile: 16 (over z, y, x), chan: 2 (over core).
Axes of the slice: x: 2, y: 2, z: 4, core: 2. Of those that a mesh axis runs over, the one named last changes fastest.
Arguments:
- panels: bfloat16 [64, 2, 256, 256], P('tile', 'chan'), may hold values from -6 to 6
- pair_ends: int32 [128, 2], P('tile'), may hold values from 0 to 63, as said below
- peaks: int32 [128, 8, 2], P(('tile', 'chan')), may hold values from 0 to 255
Outputs:
- surface: bfloat16 [128, 256, 256], P(('tile', 'chan'))
- scores: float32 [128, 8], P(('tile', 'chan'))
The draws below stay inside these ranges and needn't reach their ends.
Inputs may be any that keep to these rules, and one draw needn't show every extreme that they name: `pair_ends`: rows p * 8 to (p + 1) * 8 - 1 belong to tile index p: their column 0 is a tile of that index's block of 4 tiles, column 1 another tile whose block is at most 2 indices away; distances 2 and -2 both occur.
All inputs are finite; a program needn't handle non-finite values.
Results may differ from the reference program's by a relative error of at most 0.017.
Values may be sent and summed in bfloat16 or wider, within the bound.
No kernel may reach another device: no remote copies, remote signals or barrier semaphores. Data moves between devices by JAX's collectives and lax.ppermute only.
A program may use at most 64 MiB of HBM per device.

```python
import math
import jax
import jax.numpy as jnp
from jax import lax

N = 256
TILE_DEV = 4
REACH = 2
CAND = 8
TILES = 64
CHAN = 2
PAIR_DEV = 8
PAIRS = 128


def draw_pair_ends(key, part):
    key = jax.random.fold_in(key, 11)
    key_first, key_offset, key_second, key_other = jax.random.split(key, 4)
    tile_count = TILES // TILE_DEV
    position = jnp.arange(PAIRS, dtype=jnp.int32)
    owner = position // PAIR_DEV
    first_local = jax.random.randint(key_first, (PAIRS,), 0, TILE_DEV)
    offset = jax.random.randint(key_offset, (PAIRS,), -REACH, REACH + 1)
    offset = jnp.where(position == REACH * PAIR_DEV, REACH, offset)
    offset = jnp.where(position == REACH * PAIR_DEV + 1, -REACH, offset)
    home = owner + offset
    home = jnp.where((home < 0) | (home >= tile_count), owner - offset, home)
    second_local = jax.random.randint(key_second, (PAIRS,), 0, TILE_DEV)
    other_local = (first_local + 1 + jax.random.randint(key_other, (PAIRS,), 0, TILE_DEV - 1)) % TILE_DEV
    second_local = jnp.where(home == owner, other_local, second_local)
    first_tile = owner * TILE_DEV + first_local
    second_tile = home * TILE_DEV + second_local
    return jnp.stack([first_tile, second_tile], axis=1).astype(jnp.int32)


def plant(entries, stream_key, low, top_value):
    dims = entries.shape
    spot = [jax.random.randint(jax.random.fold_in(stream_key, axis), (), 0, dims[axis]) for axis in range(len(dims))]
    entries = entries.at[tuple(spot)].set(low)
    longest = dims.index(max(dims))
    spot[longest] = (spot[longest] + 1) % dims[longest]
    return entries.at[tuple(spot)].set(top_value)


def levels(own_key, shape, pieces, low, largest):
    def one(dim, parts):
        draws = jax.random.uniform(jax.random.fold_in(jax.random.fold_in(own_key, 6), dim), (parts,), jnp.float32, low / len(pieces), largest / len(pieces))
        return jnp.repeat(jnp.exp(draws), shape[dim] // parts).reshape((-1,) + (1,) * (len(shape) - dim - 1))

    factor_of = one(*pieces[0])
    for cut in pieces[1:]:
        factor_of = factor_of * one(*cut)
    return factor_of


def normal_values(stream_key, shape, deviation, bound, cuts=(), kind=jnp.bfloat16):
    drawn = jax.random.normal(stream_key, shape, jnp.float32) * deviation
    if len(cuts) > 0:
        drawn = levels(stream_key, shape, cuts, -0.22, 0.18) * drawn
    return jnp.clip(drawn, min=-bound, max=bound).astype(kind)


def setup_inputs(seed: int = 0) -> dict:
    splits = jax.random.split(jax.random.key(seed), 4)
    return {
        "panels": normal_values(splits[0], (TILES, CHAN, N, N), 1.0, 6.0, ((0, 16), (1, 2))),
        "pair_ends": draw_pair_ends(jax.random.fold_in(splits[3], 71), 0),
        "peaks": plant(jax.random.randint(splits[2], (PAIRS, CAND, 2), 0, N), jax.random.fold_in(splits[2], 1), 0, N - 1).astype(jnp.int32),
    }


SIGMA = 0.5
FLOOR = 0.05

def fourier_tables(size):
    index = jnp.arange(size, dtype=jnp.int32)
    product = index[:, None] * index[None, :] % size
    angle = product.astype(jnp.float32) * (2.0 * math.pi / size)
    return (jnp.cos(angle).astype(jnp.bfloat16), jnp.sin(angle).astype(jnp.bfloat16))

def gauss_table(size):
    index = jnp.arange(size, dtype=jnp.float32)
    offset = index[:, None] - index[None, :]
    weight = jnp.exp(-offset * offset / (2.0 * SIGMA * SIGMA))
    return (weight / lax.optimization_barrier(jnp.sum(weight, axis=1, keepdims=True))).astype(jnp.bfloat16)

def spectrum_one(panel, gauss, cosine, sine):
    size = panel.shape[-1]
    first = jnp.dot(panel, gauss.T, preferred_element_type=jnp.float32).astype(jnp.bfloat16)
    smooth = jnp.dot(gauss, first, preferred_element_type=jnp.float32).astype(jnp.bfloat16)
    part_real = jnp.dot(smooth, cosine, preferred_element_type=jnp.float32).astype(jnp.bfloat16)
    part_imag = (-jnp.dot(smooth, sine, preferred_element_type=jnp.float32)).astype(jnp.bfloat16)
    spec_real = (jnp.dot(cosine, part_real, preferred_element_type=jnp.float32) + jnp.dot(sine, part_imag, preferred_element_type=jnp.float32)) / size
    spec_imag = (jnp.dot(cosine, part_imag, preferred_element_type=jnp.float32) - jnp.dot(sine, part_real, preferred_element_type=jnp.float32)) / size
    return (spec_real, spec_imag)

def reference(panels, pair_ends, peaks):
    size = panels.shape[-1]
    cosine, sine = fourier_tables(size)
    gauss = gauss_table(size)

    def per_tile(tile_panels):

        def per_channel(panel):
            return spectrum_one(panel, gauss, cosine, sine)
        return jax.vmap(per_channel)(tile_panels)
    real_all, imag_all = lax.map(per_tile, panels)

    def one_pair(item):
        ends, peak = item
        real_a = real_all[ends[0]]
        imag_a = imag_all[ends[0]]
        real_b = real_all[ends[1]]
        imag_b = imag_all[ends[1]]
        cross_real = lax.optimization_barrier(jnp.sum(real_a * real_b + imag_a * imag_b, axis=0))
        cross_imag = lax.optimization_barrier(jnp.sum(imag_a * real_b - real_a * imag_b, axis=0))
        magnitude = jnp.sqrt(cross_real * cross_real + cross_imag * cross_imag)
        level = jnp.mean(magnitude) + 1e-06
        denom = magnitude + FLOOR * level
        q_real = (cross_real / denom).astype(jnp.bfloat16)
        q_imag = (cross_imag / denom).astype(jnp.bfloat16)
        y_real = (jnp.dot(q_real, cosine, preferred_element_type=jnp.float32) - jnp.dot(q_imag, sine, preferred_element_type=jnp.float32)).astype(jnp.bfloat16)
        y_imag = (jnp.dot(q_real, sine, preferred_element_type=jnp.float32) + jnp.dot(q_imag, cosine, preferred_element_type=jnp.float32)).astype(jnp.bfloat16)
        corr = (jnp.dot(cosine, y_real, preferred_element_type=jnp.float32) - jnp.dot(sine, y_imag, preferred_element_type=jnp.float32)) / size
        scores = corr[peak[:, 0], peak[:, 1]]
        return (corr.astype(jnp.bfloat16), scores)
    surface, scores = lax.map(one_pair, (pair_ends, peaks))
    return (surface, scores)
```

```python
import functools
import math

import jax
import jax.numpy as jnp
import ml_dtypes
import numpy as np
from jax import lax
from jax.experimental import pallas as pl
from jax.experimental.pallas import tpu as pltpu
from jax.sharding import PartitionSpec as P

SIGMA = 0.5
FLOOR = 0.05
PLANE = 4
EXTRA = 16
BOTH = ("tile", "chan")
VMEM = pl.BlockSpec(memory_space=pltpu.VMEM)
SMEM = pl.BlockSpec(memory_space=pltpu.SMEM)
ANY = pl.BlockSpec(memory_space=pl.ANY)


def tables(size):
    index = np.arange(size)
    angle = (index[:, None] * index[None, :] % size) * (2.0 * math.pi / size)
    cosine = np.cos(angle).astype(ml_dtypes.bfloat16).astype(np.float64)
    sine = np.sin(angle).astype(ml_dtypes.bfloat16).astype(np.float64)
    offset = index[:, None] - index[None, :]
    weight = np.exp(-offset * offset / (2.0 * SIGMA * SIGMA))
    gauss = weight / weight.sum(axis=1, keepdims=True)
    half = size // 2
    columns = np.concatenate([cosine, -sine], axis=1)
    pad = np.zeros((EXTRA - 1, 2 * size))
    real = np.concatenate([cosine, sine], axis=1) / size
    imag = np.concatenate([-sine, cosine], axis=1) / size
    rows = np.concatenate([real[:half], imag[:half], real[half : half + 1], pad, imag[half : half + 1], pad], axis=0)
    back = np.block([[cosine, sine], [-sine, cosine]])
    twice = np.full((1, half), 2.0)
    twice[0, 0] = 1.0
    sines = -sine[:, :half] * twice
    sines[:, 0] = cosine[:, half]
    last = np.concatenate([cosine[:, :half] * twice, sines], axis=1) / size
    return [jnp.asarray(t.astype(ml_dtypes.bfloat16)) for t in (gauss.T, gauss, columns, rows, back, last)]


def product(left, right):
    return jnp.dot(left, right, preferred_element_type=jnp.float32)


def spectrum(panel, gauss_t, gauss, columns, rows):
    size = panel.shape[-1]
    first = product(panel, gauss_t[...]).astype(jnp.bfloat16)
    smooth = product(gauss[...], first).astype(jnp.bfloat16)
    part = product(smooth, columns[...]).astype(jnp.bfloat16)
    return product(rows[...], jnp.concatenate([part[:, :size], part[:, size:]], axis=0))


def local_kernel(panels, gauss_t, gauss, columns, rows, out):
    for tile in range(panels.shape[0]):
        out[tile] = spectrum(panels[tile], gauss_t, gauss, columns, rows)


def split(slab, half):
    return (slab[:half], slab[half : 2 * half], slab[2 * half : 2 * half + EXTRA], slab[2 * half + EXTRA :])


def cross_kernel(mine, ends, panels, *refs):
    blocks, (spectra, gauss_t, gauss, columns, rows, out, taken, sems) = refs[:5], refs[5:]
    here = lax.axis_index("tile")
    chan = lax.axis_index("chan")
    tile_dev = panels.shape[0]
    half = panels.shape[-1] // 2
    count = out.shape[0]
    first_pair = count * (chan if mine else 1 - chan)
    place = here % PLANE
    outer = (place == 0) | (place == 3)
    one = jnp.where(place % 2 == 0, 1, -1)
    two = jnp.where(place < 2, 2, -2)
    copies = []
    for k in range(count):
        tile = ends[2 * (first_pair + k) + 1]
        away = tile // tile_dev - here
        slot = tile % tile_dev
        even = chan == 0
        by_x = away == one
        by_y = away == two
        by_z = away == -two
        by_d = away == -one
        picks = [
            (away == 0, panels),
            ((by_y & even) | (by_x & ~even), blocks[0]),
            ((by_x & even) | (by_y & ~even), blocks[1]),
            (by_z & even, blocks[2]),
            (by_d, blocks[3]),
            (by_z & ~even, blocks[4]),
        ]
        for pick, source in picks:

            @pl.when(pick)
            def _(source=source):
                pltpu.make_async_copy(source.at[slot], taken.at[k], sems.at[k]).start()

    for k in range(count):
        pltpu.make_async_copy(panels.at[0], taken.at[k], sems.at[k]).wait()
        b_real, b_imag, b_real_x, b_imag_x = split(spectrum(taken[k], gauss_t, gauss, columns, rows), half)
        a = spectra.at[ends[2 * (first_pair + k)] - here * tile_dev]
        a_real, a_imag, a_real_x, a_imag_x = split(a[...], half)
        out[k] = jnp.concatenate(
            [
                a_real * b_real + a_imag * b_imag,
                a_imag * b_real - a_real * b_imag,
                a_real_x * b_real_x + a_imag_x * b_imag_x,
                a_imag_x * b_real_x - a_real_x * b_imag_x,
            ],
            axis=0,
        ).astype(jnp.bfloat16)


def surface_kernel(peaks, mine, other, peak_columns, back, last, surface, scores, corr):
    count, _, size = surface.shape
    cand = scores.shape[1]
    half = size // 2
    for k in range(count):
        slab = mine[k].astype(jnp.float32) + other[k].astype(jnp.float32)
        real, imag, real_x, imag_x = split(slab, half)
        magnitude = jnp.sqrt(real * real + imag * imag)
        magnitude_x = jnp.sqrt(real_x * real_x + imag_x * imag_x)
        total = 2.0 * jnp.sum(magnitude) - jnp.sum(magnitude[:1]) + jnp.sum(magnitude_x)
        level = total / (size * size) + 1e-06
        scale = 1.0 / (magnitude + FLOOR * level)
        scale_x = 1.0 / (magnitude_x + FLOOR * level)
        q_real = jnp.concatenate([real * scale, real_x * scale_x], axis=0)
        q_imag = jnp.concatenate([imag * scale, imag_x * scale_x], axis=0)
        q = jnp.concatenate([q_real, q_imag], axis=1).astype(jnp.bfloat16)
        y = product(q, back[...])
        y_real = y[:half, :size]
        y_imag = y[:half, size:]
        row = lax.broadcasted_iota(jnp.int32, y_imag.shape, 0)
        y_imag = jnp.where(row == 0, y[half : half + 1, :size], y_imag)
        both = jnp.concatenate([y_real, y_imag], axis=0).astype(jnp.bfloat16)
        result = product(last[...], both)
        corr[k] = result
        surface[k] = result.astype(jnp.bfloat16)
    lane = lax.broadcasted_iota(jnp.int32, (cand, size), 1)
    diagonal = lax.broadcasted_iota(jnp.int32, (cand, cand), 0) == lax.broadcasted_iota(jnp.int32, (cand, cand), 1)
    for k in range(count):
        picked = jnp.concatenate([corr[k, pl.ds(peaks[k * cand + j], 1), :] for j in range(cand)], axis=0)
        found = jnp.sum(jnp.where(lane == peak_columns[k], picked, 0.0), axis=1, keepdims=True)
        scores[k : k + 1, :] = jnp.sum(jnp.where(diagonal, found, 0.0), axis=0, keepdims=True)


def routes(devices):
    def up(t, c):
        return (t + PLANE, c) if t + PLANE < devices else (t, 1 - c)

    def down(t, c):
        return (t - PLANE, c) if t >= PLANE else (t, 1 - c)

    def across(c, core):
        return 2 if c == core else 1

    def pairs(step):
        return [(2 * t + c, 2 * d + e) for t in range(devices) for c in range(2) for d, e in [step(t, c)]]

    return (
        pairs(lambda t, c: (t ^ across(c, 0), c)),
        pairs(lambda t, c: (t ^ across(c, 1), c)),
        pairs(lambda t, c: (up if (t % PLANE < 2) == (c == 0) else down)(t, c)),
        pairs(lambda t, c: (t ^ across(c, 1), c)),
        pairs(lambda t, c: (up if (t % PLANE < 2) == (c == 1) else down)(t, c)),
    )


def after(value, earlier):
    return lax.optimization_barrier((value, earlier))[0]


def shards(panels, pair_ends, peaks):
    tile_dev, _, size, _ = panels.shape
    share, cand, _ = peaks.shape
    devices = lax.axis_size("tile")
    local = panels[:, 0]
    gauss_t, gauss, columns, rows, back, last = tables(size)
    slab = size + 2 * EXTRA
    place = lax.axis_index("tile") % PLANE
    outer = (place == 0) | (place == 3)
    swap, cross_swap, climb, relay, climb_late = routes(devices)
    move = functools.partial(lax.ppermute, axis_name=BOTH)
    got_swap = move(local, perm=swap)
    got_climb = move(got_swap, perm=climb)
    got_cross = move(after(local, got_swap), perm=cross_swap)
    got_relay = move(jnp.where(outer, got_swap, got_climb), perm=relay)
    got_late = move(got_cross, perm=climb_late)
    blocks = (got_swap, got_cross, got_climb, got_relay, got_late)
    ends = pair_ends.reshape(-1)
    spectra = pl.pallas_call(
        local_kernel,
        out_shape=jax.ShapeDtypeStruct((tile_dev, slab, size), jnp.float32),
        in_specs=[VMEM] * 5,
        out_specs=VMEM,
        compiler_params=pltpu.CompilerParams(vmem_limit_bytes=32 << 20),
        cost_estimate=pl.CostEstimate(flops=tile_dev * 12 * size**3, bytes_accessed=4 << 20, transcendentals=0),
        name="local_spectra",
    )(local, gauss_t, gauss, columns, rows)

    def cross(mine):
        return pl.pallas_call(
            functools.partial(cross_kernel, mine),
            out_shape=jax.ShapeDtypeStruct((share, slab, size), jnp.bfloat16),
            in_specs=[SMEM] + [ANY] * 6 + [VMEM] * 5,
            out_specs=VMEM,
            scratch_shapes=[pltpu.VMEM((share, size, size), jnp.bfloat16), pltpu.SemaphoreType.DMA((share,))],
            compiler_params=pltpu.CompilerParams(vmem_limit_bytes=32 << 20),
            cost_estimate=pl.CostEstimate(flops=share * 12 * size**3, bytes_accessed=4 << 20, transcendentals=0),
            name="cross_mine" if mine else "cross_other",
        )(ends, local, *blocks, spectra, gauss_t, gauss, columns, rows)

    given = cross(False)
    other = lax.ppermute(given, "chan", [(0, 1), (1, 0)])
    kept = cross(True)
    surface, scores = pl.pallas_call(
        surface_kernel,
        out_shape=(
            jax.ShapeDtypeStruct((share, size, size), jnp.bfloat16),
            jax.ShapeDtypeStruct((share, cand), jnp.float32),
        ),
        in_specs=[SMEM] + [VMEM] * 5,
        out_specs=(VMEM, VMEM),
        scratch_shapes=[pltpu.VMEM((share, size, size), jnp.float32)],
        compiler_params=pltpu.CompilerParams(vmem_limit_bytes=32 << 20),
        cost_estimate=pl.CostEstimate(flops=share * 12 * size**3, bytes_accessed=4 << 20, transcendentals=0),
        name="surface",
    )(peaks[:, :, 0].reshape(-1), kept, other, peaks[:, :, 1:], back, last)
    return (surface, scores)


def solution(mesh):
    in_specs = (P("tile", "chan", None, None), P("tile", None), P(BOTH, None, None))
    out_specs = (P(BOTH, None, None), P(BOTH, None))
    return jax.shard_map(shards, mesh=mesh, in_specs=in_specs, out_specs=out_specs, check_vma=False)
```

```python
import functools
import math

import jax
import jax.numpy as jnp
import ml_dtypes
import numpy as np
from jax import lax
from jax.experimental import pallas as pl
from jax.experimental.pallas import tpu as pltpu
from jax.sharding import PartitionSpec as P

SIGMA = 0.5
FLOOR = 0.05
PLANE = 4
EXTRA = 16
BOTH = ("tile", "chan")
VMEM = pl.BlockSpec(memory_space=pltpu.VMEM)
SMEM = pl.BlockSpec(memory_space=pltpu.SMEM)


def tables(size):
    index = np.arange(size)
    angle = (index[:, None] * index[None, :] % size) * (2.0 * math.pi / size)
    cosine = np.cos(angle).astype(ml_dtypes.bfloat16).astype(np.float64)
    sine = np.sin(angle).astype(ml_dtypes.bfloat16).astype(np.float64)
    offset = index[:, None] - index[None, :]
    weight = np.exp(-offset * offset / (2.0 * SIGMA * SIGMA))
    gauss = weight / weight.sum(axis=1, keepdims=True)
    half = size // 2
    columns = np.concatenate([cosine, -sine], axis=1)
    pad = np.zeros((EXTRA - 1, 2 * size))
    real = np.concatenate([cosine, sine], axis=1) / size
    imag = np.concatenate([-sine, cosine], axis=1) / size
    rows = np.concatenate([real[:half], imag[:half], real[half : half + 1], pad, imag[half : half + 1], pad], axis=0)
    back = np.block([[cosine, sine], [-sine, cosine]])
    twice = np.full((1, half), 2.0)
    twice[0, 0] = 1.0
    sines = -sine[:, :half] * twice
    sines[:, 0] = cosine[:, half]
    last = np.concatenate([cosine[:, :half] * twice, sines], axis=1) / size
    wide = np.concatenate([gauss.T, gauss], axis=1)
    narrow = np.concatenate([last, np.zeros((size, size))], axis=1)
    return jnp.asarray(np.concatenate([wide, columns, back, narrow, rows], axis=0).astype(ml_dtypes.bfloat16))


def product(left, right):
    return jnp.dot(left, right, preferred_element_type=jnp.float32)


def spectra_of(panels, table):
    count, size, _ = panels.shape
    first = product(panels.reshape(count * size, size), table[:size, :size]).astype(jnp.bfloat16)
    gauss = table[:size, size:]
    smooth = [product(gauss, first[k * size : (k + 1) * size]).astype(jnp.bfloat16) for k in range(count)]
    part = product(jnp.concatenate(smooth, axis=0), table[size : 2 * size]).astype(jnp.bfloat16)
    rows = table[5 * size :]
    slabs = []
    for k in range(count):
        one = part[k * size : (k + 1) * size]
        slabs.append(product(rows, jnp.concatenate([one[:, :size], one[:, size:]], axis=0)))
    return slabs


def local_kernel(panels, table, out):
    for k, slab in enumerate(spectra_of(panels[...], table)):
        out[k] = slab


def split(slab, half):
    return (slab[:half], slab[half : 2 * half], slab[2 * half : 2 * half + EXTRA], slab[2 * half + EXTRA :])


def cross_kernel(mine, ends, panels, *refs):
    blocks, (spectra, table, out, taken) = refs[:5], refs[5:]
    here = lax.axis_index("tile")
    chan = lax.axis_index("chan")
    tile_dev = panels.shape[0]
    half = panels.shape[-1] // 2
    count = out.shape[0]
    first_pair = count * (chan if mine else 1 - chan)
    place = here % PLANE
    one = jnp.where(place % 2 == 0, 1, -1)
    two = jnp.where(place < 2, 2, -2)
    even = chan == 0
    held = (0, jnp.where(even, two, one), jnp.where(even, one, two), jnp.where(even, -two, 0), -one, jnp.where(even, 0, -two))
    for k in range(count):
        tile = ends[2 * (first_pair + k) + 1]
        away = tile // tile_dev - here
        slot = tile % tile_dev
        for index, (distance, source) in enumerate(zip(held, (panels, *blocks))):

            @pl.when(away == distance if index in (0, 1, 2, 4) else (away == distance) & (distance != 0))
            def _(source=source):
                taken[k] = source[slot]

    for k, slab in enumerate(spectra_of(taken[...], table)):
        b_real, b_imag, b_real_x, b_imag_x = split(slab, half)
        a = spectra.at[ends[2 * (first_pair + k)] - here * tile_dev]
        a_real, a_imag, a_real_x, a_imag_x = split(a[...], half)
        out[k] = jnp.concatenate(
            [
                a_real * b_real + a_imag * b_imag,
                a_imag * b_real - a_real * b_imag,
                a_real_x * b_real_x + a_imag_x * b_imag_x,
                a_imag_x * b_real_x - a_real_x * b_imag_x,
            ],
            axis=0,
        ).astype(jnp.bfloat16)


def surface_kernel(peaks, mine, other, peak_columns, table, surface, scores, corr):
    count, _, size = surface.shape
    cand = scores.shape[1]
    half = size // 2
    parts = []
    for k in range(count):
        slab = mine[k].astype(jnp.float32) + other[k].astype(jnp.float32)
        real, imag, real_x, imag_x = split(slab, half)
        magnitude = jnp.sqrt(real * real + imag * imag)
        magnitude_x = jnp.sqrt(real_x * real_x + imag_x * imag_x)
        total = 2.0 * jnp.sum(magnitude) - jnp.sum(magnitude[:1]) + jnp.sum(magnitude_x)
        level = total / (size * size) + 1e-06
        scale = 1.0 / (magnitude + FLOOR * level)
        scale_x = 1.0 / (magnitude_x + FLOOR * level)
        q_real = jnp.concatenate([real * scale, real_x * scale_x], axis=0)
        q_imag = jnp.concatenate([imag * scale, imag_x * scale_x], axis=0)
        parts.append(jnp.concatenate([q_real, q_imag], axis=1).astype(jnp.bfloat16))
    spread = half + EXTRA
    y_all = product(jnp.concatenate(parts, axis=0), table[2 * size : 4 * size])
    last = table[4 * size : 5 * size, :size]
    for k in range(count):
        y = y_all[k * spread : (k + 1) * spread]
        y_real = y[:half, :size]
        y_imag = y[:half, size:]
        row = lax.broadcasted_iota(jnp.int32, y_imag.shape, 0)
        y_imag = jnp.where(row == 0, y[half : half + 1, :size], y_imag)
        both = jnp.concatenate([y_real, y_imag], axis=0).astype(jnp.bfloat16)
        result = product(last, both)
        corr[k] = result
        surface[k] = result.astype(jnp.bfloat16)
    lane = lax.broadcasted_iota(jnp.int32, (cand, size), 1)
    diagonal = lax.broadcasted_iota(jnp.int32, (cand, cand), 0) == lax.broadcasted_iota(jnp.int32, (cand, cand), 1)
    for k in range(count):
        picked = jnp.concatenate([corr[k, pl.ds(peaks[k * cand + j], 1), :] for j in range(cand)], axis=0)
        found = jnp.sum(jnp.where(lane == peak_columns[k], picked, 0.0), axis=1, keepdims=True)
        scores[k : k + 1, :] = jnp.sum(jnp.where(diagonal, found, 0.0), axis=0, keepdims=True)


def routes(devices):
    def up(t, c):
        return (t + PLANE, c) if t + PLANE < devices else (t, 1 - c)

    def down(t, c):
        return (t - PLANE, c) if t >= PLANE else (t, 1 - c)

    def across(c, core):
        return 2 if c == core else 1

    def pairs(step):
        return [(2 * t + c, 2 * d + e) for t in range(devices) for c in range(2) for d, e in [step(t, c)]]

    return (
        pairs(lambda t, c: (t ^ across(c, 0), c)),
        pairs(lambda t, c: (t ^ across(c, 1), c)),
        pairs(lambda t, c: (up if (t % PLANE < 2) == (c == 0) else down)(t, c)),
        pairs(lambda t, c: (t ^ across(c, 1), c)),
        pairs(lambda t, c: (up if (t % PLANE < 2) == (c == 1) else down)(t, c)),
    )


def after(value, *earlier):
    return lax.optimization_barrier((value, *earlier))[0]


def call(kernel, name, operands, scalars, out, scratch=()):
    return pl.pallas_call(
        kernel,
        out_shape=out,
        in_specs=[SMEM] * scalars + [VMEM] * (len(operands) - scalars),
        out_specs=jax.tree.map(lambda _: VMEM, out),
        scratch_shapes=scratch,
        compiler_params=pltpu.CompilerParams(vmem_limit_bytes=16 << 20),
        cost_estimate=pl.CostEstimate(flops=1 << 30, bytes_accessed=4 << 20, transcendentals=0),
        name=name,
    )(*operands)


def shards(panels, pair_ends, peaks):
    tile_dev, _, size, _ = panels.shape
    share, cand, _ = peaks.shape
    devices = lax.axis_size("tile")
    local = panels[:, 0]
    table = tables(size)
    slab = size + 2 * EXTRA
    place = lax.axis_index("tile") % PLANE
    outer = (place == 0) | (place == 3)
    swap, cross_swap, climb, relay, climb_late = routes(devices)
    move = functools.partial(lax.ppermute, axis_name=BOTH)
    ends = pair_ends.reshape(-1)
    peak_rows = peaks[:, :, 0].reshape(-1)
    peak_columns = peaks[:, :, 1:]
    got_swap = move(local, perm=swap)
    spectra = call(local_kernel, "local_spectra", (local, table), 0, jax.ShapeDtypeStruct((tile_dev, slab, size), jnp.float32))
    got_climb = move(got_swap, perm=climb)
    got_cross = move(after(local, spectra, ends, peak_rows, peak_columns), perm=cross_swap)
    got_relay = move(jnp.where(outer, got_swap, got_climb), perm=relay)
    got_late = move(got_cross, perm=climb_late)
    blocks = (got_swap, got_cross, got_climb, got_relay, got_late)

    def cross(mine):
        return call(
            functools.partial(cross_kernel, mine),
            "cross_mine" if mine else "cross_other",
            (ends, local, *blocks, spectra, table),
            1,
            jax.ShapeDtypeStruct((share, slab, size), jnp.bfloat16),
            [pltpu.VMEM((share, size, size), jnp.bfloat16)],
        )

    given = cross(False)
    other = lax.ppermute(given, "chan", [(0, 1), (1, 0)])
    kept = cross(True)
    surface, scores = call(
        surface_kernel,
        "surface",
        (peak_rows, kept, other, peak_columns, table),
        1,
        (jax.ShapeDtypeStruct((share, size, size), jnp.bfloat16), jax.ShapeDtypeStruct((share, cand), jnp.float32)),
        [pltpu.VMEM((share, size, size), jnp.float32)],
    )
    return (surface, scores)


def solution(mesh):
    in_specs = (P("tile", "chan", None, None), P("tile", None), P(BOTH, None, None))
    out_specs = (P(BOTH, None, None), P(BOTH, None))
    return jax.shard_map(shards, mesh=mesh, in_specs=in_specs, out_specs=out_specs, check_vma=False)
```

```python
import functools
import math

import jax
import jax.numpy as jnp
import ml_dtypes
import numpy as np
from jax import lax
from jax.experimental import pallas as pl
from jax.experimental.pallas import tpu as pltpu
from jax.sharding import PartitionSpec as P

SIGMA = 0.5
FLOOR = 0.05
PLANE = 4
EXTRA = 16
CUT2 = True
VLIM = 8
BOTH = ("tile", "chan")
VMEM = pl.BlockSpec(memory_space=pltpu.VMEM)
SMEM = pl.BlockSpec(memory_space=pltpu.SMEM)


def tables(size):
    index = np.arange(size)
    angle = (index[:, None] * index[None, :] % size) * (2.0 * math.pi / size)
    cosine = np.cos(angle).astype(ml_dtypes.bfloat16).astype(np.float64)
    sine = np.sin(angle).astype(ml_dtypes.bfloat16).astype(np.float64)
    offset = index[:, None] - index[None, :]
    weight = np.exp(-offset * offset / (2.0 * SIGMA * SIGMA))
    gauss = weight / weight.sum(axis=1, keepdims=True)
    half = size // 2
    columns = np.concatenate([cosine, -sine], axis=1)
    pad = np.zeros((EXTRA - 1, 2 * size))
    real = np.concatenate([cosine, sine], axis=1) / size
    imag = np.concatenate([-sine, cosine], axis=1) / size
    rows = np.concatenate([real[:half], imag[:half], real[half : half + 1], pad, imag[half : half + 1], pad], axis=0)
    back = np.block([[cosine, sine], [-sine, cosine]])
    twice = np.full((1, half), 2.0)
    twice[0, 0] = 1.0
    sines = -sine[:, :half] * twice
    sines[:, 0] = cosine[:, half]
    last = np.concatenate([cosine[:, :half] * twice, sines], axis=1) / size
    wide = np.concatenate([gauss.T, gauss], axis=1)
    narrow = np.concatenate([last, np.zeros((size, size))], axis=1)
    return jnp.asarray(np.concatenate([wide, columns, back, narrow, rows], axis=0).astype(ml_dtypes.bfloat16))


def product(left, right):
    return jnp.dot(left, right, preferred_element_type=jnp.float32)


def spectra_of(panels, table):
    count, size, _ = panels.shape
    first = product(panels.reshape(count * size, size), table[:size, :size]).astype(jnp.bfloat16)
    gauss = table[:size, size:]
    smooth = [product(gauss, first[k * size : (k + 1) * size]).astype(jnp.bfloat16) for k in range(count)]
    part = product(jnp.concatenate(smooth, axis=0), table[size : 2 * size]).astype(jnp.bfloat16)
    rows = table[5 * size :]
    slabs = []
    for k in range(count):
        one = part[k * size : (k + 1) * size]
        slabs.append(product(rows, jnp.concatenate([one[:, :size], one[:, size:]], axis=0)))
    return slabs


def local_kernel(*refs):
    panels, (table, out) = refs[:-2], refs[-2:]
    for k, slab in enumerate(spectra_of(jnp.concatenate([p[...] for p in panels], axis=0), table)):
        out[k] = slab


def split(slab, half):
    return (slab[:half], slab[half : 2 * half], slab[2 * half : 2 * half + EXTRA], slab[2 * half + EXTRA :])


def distances(here, chan):
    place = here % PLANE
    one = jnp.where(place % 2 == 0, 1, -1)
    two = jnp.where(place < 2, 2, -2)
    even = chan == 0
    never = 2 * PLANE
    return (
        0,
        jnp.where(even, two, one),
        jnp.where(even, one, two),
        jnp.where(even, -two, never),
        jnp.where(even, never, -two),
        -one,
    )


def cross_slab(a_slab, b_slab, half):
    a_real, a_imag, a_real_x, a_imag_x = split(a_slab, half)
    b_real, b_imag, b_real_x, b_imag_x = split(b_slab, half)
    parts = [
        a_real * b_real + a_imag * b_imag,
        a_imag * b_real - a_real * b_imag,
        a_real_x * b_real_x + a_imag_x * b_imag_x,
        a_imag_x * b_real_x - a_real_x * b_imag_x,
    ]
    return jnp.concatenate(parts, axis=0).astype(jnp.bfloat16)


def early_kernel(cuts, ends, *refs):
    blocks, (spectra, table, other, mine, taken) = refs[: len(cuts)], refs[len(cuts) :]
    here = lax.axis_index("tile")
    chan = lax.axis_index("chan")
    held = distances(here, chan)
    tile_dev = spectra.shape[0]
    half = taken.shape[-1] // 2
    for out, owner in ((other, 1 - chan), (mine, chan)):
        count = out.shape[0]
        for k in range(count):
            tile = ends[1, owner * count + k]
            away = tile // tile_dev - here
            slot = tile % tile_dev
            for (index, base), source in zip(cuts, blocks):
                size = source.shape[0]
                pick = away == held[index]
                if size < tile_dev:
                    pick = pick & (slot >= base) & (slot < base + size)

                @pl.when(pick)
                def _(source=source, base=base):
                    taken[k] = source[slot - base]

        for k, slab in enumerate(spectra_of(taken[...], table)):
            own = ends[0, owner * count + k] - here * tile_dev
            out[k] = cross_slab(spectra[own], slab, half)


def late_kernel(mine, ends, *refs):
    blocks, (early, spectra, table, out, taken) = refs[:-5], refs[-5:]
    here = lax.axis_index("tile")
    chan = lax.axis_index("chan")
    last = distances(here, chan)[-1]
    tile_dev = spectra.shape[0]
    half = taken.shape[-1] // 2
    count = out.shape[0]
    out[...] = early[...]

    @pl.loop(0, count)
    def _(k):
        pair = count * (chan if mine else 1 - chan) + k
        tile = ends[1, pair]
        slot = tile % tile_dev

        @pl.when(tile // tile_dev - here == last)
        def _():
            base = 0
            for source in blocks:
                size = source.shape[0]

                @pl.when((slot >= base) & (slot < base + size))
                def _(source=source, base=base):
                    taken[0] = source[slot - base]

                base += size
            (slab,) = spectra_of(taken[...], table)
            out[k] = cross_slab(spectra[ends[0, pair] - here * tile_dev], slab, half)


def surface_kernel(peaks, mine, other, table, surface, scores, corr):
    count, _, size = surface.shape
    cand = scores.shape[1]
    half = size // 2
    parts = []
    for k in range(count):
        slab = mine[k].astype(jnp.float32) + other[k].astype(jnp.float32)
        real, imag, real_x, imag_x = split(slab, half)
        magnitude = jnp.sqrt(real * real + imag * imag)
        magnitude_x = jnp.sqrt(real_x * real_x + imag_x * imag_x)
        total = 2.0 * jnp.sum(magnitude) - jnp.sum(magnitude[:1]) + jnp.sum(magnitude_x)
        level = total / (size * size) + 1e-06
        scale = 1.0 / (magnitude + FLOOR * level)
        scale_x = 1.0 / (magnitude_x + FLOOR * level)
        q_real = jnp.concatenate([real * scale, real_x * scale_x], axis=0)
        q_imag = jnp.concatenate([imag * scale, imag_x * scale_x], axis=0)
        parts.append(jnp.concatenate([q_real, q_imag], axis=1).astype(jnp.bfloat16))
    spread = half + EXTRA
    y_all = product(jnp.concatenate(parts, axis=0), table[2 * size : 4 * size])
    last = table[4 * size : 5 * size, :size]
    for k in range(count):
        y = y_all[k * spread : (k + 1) * spread]
        y_real = y[:half, :size]
        y_imag = y[:half, size:]
        row = lax.broadcasted_iota(jnp.int32, y_imag.shape, 0)
        y_imag = jnp.where(row == 0, y[half : half + 1, :size], y_imag)
        both = jnp.concatenate([y_real, y_imag], axis=0).astype(jnp.bfloat16)
        result = product(last, both)
        corr[k] = result
        surface[k] = result.astype(jnp.bfloat16)
    lane = lax.broadcasted_iota(jnp.int32, (1, size), 1)
    diagonal = lax.broadcasted_iota(jnp.int32, (cand, cand), 0) == lax.broadcasted_iota(jnp.int32, (cand, cand), 1)
    for k in range(count):
        picked = []
        for j in range(cand):
            row = corr[k, pl.ds(peaks[k, 0, j], 1), :]
            picked.append(jnp.where(lane == peaks[k, 1, j], row, 0.0))
        found = jnp.sum(jnp.concatenate(picked, axis=0), axis=1, keepdims=True)
        scores[k : k + 1, :] = jnp.sum(jnp.where(diagonal, found, 0.0), axis=0, keepdims=True)


def choose_kernel(first, second, out):
    place = lax.axis_index("tile") % PLANE
    outer = (place == 0) | (place == PLANE - 1)

    @pl.when(outer)
    def _():
        out[...] = first[...]

    @pl.when(jnp.logical_not(outer))
    def _():
        out[...] = second[...]


def routes(devices):
    def up(t, c):
        return (t + PLANE, c) if t + PLANE < devices else (t, 1 - c)

    def down(t, c):
        return (t - PLANE, c) if t >= PLANE else (t, 1 - c)

    def across(c, core):
        return 2 if c == core else 1

    def pairs(step):
        return [(2 * t + c, 2 * d + e) for t in range(devices) for c in range(2) for d, e in [step(t, c)]]

    return (
        pairs(lambda t, c: (t ^ across(c, 0), c)),
        pairs(lambda t, c: (t ^ across(c, 1), c)),
        pairs(lambda t, c: (up if (t % PLANE < 2) == (c == 0) else down)(t, c)),
        pairs(lambda t, c: (t ^ across(c, 1), c)),
        pairs(lambda t, c: (up if (t % PLANE < 2) == (c == 1) else down)(t, c)),
    )


def after(value, *earlier):
    return lax.optimization_barrier((value, *earlier))[0]


def call(kernel, name, operands, scalars, out, scratch=()):
    return pl.pallas_call(
        kernel,
        out_shape=out,
        in_specs=[SMEM] * scalars + [VMEM] * (len(operands) - scalars),
        out_specs=jax.tree.map(lambda _: VMEM, out),
        scratch_shapes=scratch,
        compiler_params=pltpu.CompilerParams(vmem_limit_bytes=VLIM << 20),
        cost_estimate=pl.CostEstimate(flops=1 << 30, bytes_accessed=4 << 20, transcendentals=0),
        name=name,
    )(*operands)


def shards(panels, pair_ends, peaks):
    tile_dev, _, size, _ = panels.shape
    share, cand, _ = peaks.shape
    devices = lax.axis_size("tile")
    local = panels[:, 0]
    table = tables(size)
    slab = size + 2 * EXTRA
    swap, cross_swap, climb, relay, climb_late = routes(devices)
    move = functools.partial(lax.ppermute, axis_name=BOTH)
    ends = pair_ends.T
    spots = jnp.transpose(peaks, (0, 2, 1))
    half = tile_dev // 2
    parts = [local[:half], local[half:]]

    def chosen(first, second):
        return call(choose_kernel, "choose", (first, second), 0, jax.ShapeDtypeStruct(first.shape, first.dtype))

    got_swap = [move(part, perm=swap) for part in parts]
    spectra = call(local_kernel, "local_spectra", (*parts, table), 0, jax.ShapeDtypeStruct((tile_dev, slab, size), jnp.float32))
    got_climb = [move(part, perm=climb) for part in got_swap]
    got_cross = [move(part, perm=cross_swap) for part in (after(parts, spectra) if CUT2 else [after(local, spectra)])]
    got_relay = [move(chosen(a, b), perm=relay) for a, b in zip(got_swap, got_climb)]
    got_late = [move(part, perm=climb_late) for part in got_cross]
    blocks, cuts = [], []
    for index, arrival in enumerate((parts, got_swap, got_cross, got_climb, got_late)):
        base = 0
        for part in arrival:
            blocks.append(part)
            cuts.append((index, base))
            base += part.shape[0]
    crosses = jax.ShapeDtypeStruct((share, slab, size), jnp.bfloat16)
    early_other, early_mine = call(
        functools.partial(early_kernel, cuts),
        "cross_early",
        (ends, *blocks, spectra, table),
        1,
        (crosses, crosses),
        [pltpu.VMEM((share, size, size), jnp.bfloat16)],
    )

    def late(mine, early):
        return call(
            functools.partial(late_kernel, mine),
            "cross_mine" if mine else "cross_other",
            (ends, *got_relay, early, spectra, table),
            1,
            crosses,
            [pltpu.VMEM((1, size, size), jnp.bfloat16)],
        )

    given = late(False, early_other)
    other = lax.ppermute(given, "chan", [(0, 1), (1, 0)])
    kept = late(True, early_mine)
    surface, scores = call(
        surface_kernel,
        "surface",
        (spots, kept, other, table),
        1,
        (jax.ShapeDtypeStruct((share, size, size), jnp.bfloat16), jax.ShapeDtypeStruct((share, cand), jnp.float32)),
        [pltpu.VMEM((share, size, size), jnp.float32)],
    )
    return (surface, scores)


def solution(mesh):
    in_specs = (P("tile", "chan", None, None), P("tile", None), P(BOTH, None, None))
    out_specs = (P(BOTH, None, None), P(BOTH, None))
    return jax.shard_map(shards, mesh=mesh, in_specs=in_specs, out_specs=out_specs, check_vma=False)
```

```python
import functools
import math

import jax
import jax.numpy as jnp
import ml_dtypes
import numpy as np
from jax import lax
from jax.experimental import pallas as pl
from jax.experimental.pallas import tpu as pltpu
from jax.sharding import PartitionSpec as P

SIGMA = 0.5
FLOOR = 0.05
PLANE = 4
EXTRA = 8
BOTH = ("tile", "chan")
VMEM = pl.BlockSpec(memory_space=pltpu.VMEM)
SMEM = pl.BlockSpec(memory_space=pltpu.SMEM)
ANY = pl.BlockSpec(memory_space=pl.ANY)


def tables(size):
    index = np.arange(size)
    angle = (index[:, None] * index[None, :] % size) * (2.0 * math.pi / size)
    cosine = np.cos(angle).astype(ml_dtypes.bfloat16).astype(np.float64)
    sine = np.sin(angle).astype(ml_dtypes.bfloat16).astype(np.float64)
    offset = index[:, None] - index[None, :]
    weight = np.exp(-offset * offset / (2.0 * SIGMA * SIGMA))
    gauss = weight / weight.sum(axis=1, keepdims=True)
    half = size // 2
    columns = np.concatenate([cosine, -sine], axis=1)
    pad = np.zeros((EXTRA - 1, 2 * size))
    real = np.concatenate([cosine, sine], axis=1) / size
    imag = np.concatenate([-sine, cosine], axis=1) / size
    rows = np.concatenate([real[:half], imag[:half], real[half : half + 1], pad, imag[half : half + 1], pad], axis=0)
    back = np.block([[cosine, sine], [-sine, cosine]])
    twice = np.full((1, half), 2.0)
    twice[0, 0] = 1.0
    sines = -sine[:, :half] * twice
    sines[:, 0] = cosine[:, half]
    last = np.concatenate([cosine[:, :half] * twice, sines], axis=1) / size
    wide = np.concatenate([gauss.T, gauss], axis=1)
    narrow = np.concatenate([last, np.zeros((size, size))], axis=1)
    forward = np.concatenate([wide, columns, rows], axis=0)
    backward = np.concatenate([back, narrow], axis=0)
    return jnp.asarray(forward.astype(ml_dtypes.bfloat16)), jnp.asarray(backward.astype(ml_dtypes.bfloat16))


def product(left, right):
    return jnp.dot(left, right, preferred_element_type=jnp.float32)


def spectra_of(panels, table):
    count, size, _ = panels.shape
    first = product(panels.reshape(count * size, size), table[:size, :size]).astype(jnp.bfloat16)
    gauss = table[:size, size:]
    smooth = [product(gauss, first[k * size : (k + 1) * size]).astype(jnp.bfloat16) for k in range(count)]
    part = product(jnp.concatenate(smooth, axis=0), table[size : 2 * size]).astype(jnp.bfloat16)
    rows = table[2 * size :]
    slabs = []
    for k in range(count):
        one = part[k * size : (k + 1) * size]
        slabs.append(product(rows, jnp.concatenate([one[:, :size], one[:, size:]], axis=0)))
    return slabs


def spectra_kernel(core, *refs):
    panels, (table, out) = refs[:-2], refs[-2:]

    def work():
        for k, slab in enumerate(spectra_of(jnp.concatenate([p[...] for p in panels], axis=0), table)):
            out[k] = slab

    if core is None:
        work()
    else:
        pl.when(lax.axis_index("chan") == core)(work)


def split(slab, half):
    return (slab[:half], slab[half : 2 * half], slab[2 * half : 2 * half + EXTRA], slab[2 * half + EXTRA :])


def distances(here, chan):
    place = here % PLANE
    one = jnp.where(place % 2 == 0, 1, -1)
    two = jnp.where(place < 2, 2, -2)
    even = chan == 0
    never = 2 * PLANE
    return (
        0,
        jnp.where(even, two, one),
        jnp.where(even, one, two),
        jnp.where(even, -two, never),
        jnp.where(even, never, -two),
        -one,
    )


def cross_slab(a_slab, b_slab, half):
    a_real, a_imag, a_real_x, a_imag_x = split(a_slab, half)
    b_real, b_imag, b_real_x, b_imag_x = split(b_slab, half)
    parts = [
        a_real * b_real + a_imag * b_imag,
        a_imag * b_real - a_real * b_imag,
        a_real_x * b_real_x + a_imag_x * b_imag_x,
        a_imag_x * b_real_x - a_real_x * b_imag_x,
    ]
    return jnp.concatenate(parts, axis=0).astype(jnp.bfloat16)


def write_crosses(first_pair, cuts, ends, blocks, out, taken):
    here = lax.axis_index("tile")
    held = distances(here, lax.axis_index("chan"))
    own = blocks[0]
    tile_dev = own.shape[0]
    half = taken.shape[-1] // 2
    count = out.shape[0]
    for k in range(count):
        tile = ends[1, first_pair + k]
        away = tile // tile_dev - here
        slot = tile % tile_dev
        for (index, base), source in zip(cuts, blocks):
            size = source.shape[0]
            pick = away == held[index]
            if size < tile_dev:
                pick = pick & (slot >= base) & (slot < base + size)

            @pl.when(pick)
            def _(source=source, base=base):
                taken[k] = source[slot - base]

    for k in range(count):
        out[k] = cross_slab(own[ends[0, first_pair + k] - here * tile_dev], taken[k], half)


def cross_other_kernel(cuts, ends, *refs):
    blocks, (panels, table, out, slabs, taken, numbers, sem) = refs[: len(cuts) - 1], refs[len(cuts) - 1 :]
    copy = pltpu.make_async_copy(ends, numbers, sem)
    copy.start()
    for k, slab in enumerate(spectra_of(panels[...], table)):
        slabs[k] = slab
    copy.wait()
    first_pair = out.shape[0] * (1 - lax.axis_index("chan"))
    write_crosses(first_pair, cuts, numbers, (*blocks, slabs), out, taken)


def cross_mine_kernel(cuts, ends, *refs):
    blocks, (out, taken) = refs[: len(cuts)], refs[len(cuts) :]
    write_crosses(out.shape[0] * lax.axis_index("chan"), cuts, ends, blocks, out, taken)


def surface_kernel(spots, mine, other, table, surface, scores, corr, peaks, sem):
    copy = pltpu.make_async_copy(spots, peaks, sem)
    copy.start()
    count, _, size = surface.shape
    cand = scores.shape[1]
    half = size // 2
    parts = []
    for k in range(count):
        slab = mine[k].astype(jnp.float32) + other[k].astype(jnp.float32)
        real, imag, real_x, imag_x = split(slab, half)
        magnitude = jnp.sqrt(real * real + imag * imag)
        magnitude_x = jnp.sqrt(real_x * real_x + imag_x * imag_x)
        total = 2.0 * jnp.sum(magnitude) - jnp.sum(magnitude[:1]) + jnp.sum(magnitude_x)
        level = total / (size * size) + 1e-06
        scale = 1.0 / (magnitude + FLOOR * level)
        scale_x = 1.0 / (magnitude_x + FLOOR * level)
        q_real = jnp.concatenate([real * scale, real_x * scale_x], axis=0)
        q_imag = jnp.concatenate([imag * scale, imag_x * scale_x], axis=0)
        parts.append(jnp.concatenate([q_real, q_imag], axis=1))
    spread = half + EXTRA
    y_all = product(jnp.concatenate(parts, axis=0).astype(jnp.bfloat16), table[: 2 * size])
    last = table[2 * size :, :size]
    for k in range(count):
        y = y_all[k * spread : (k + 1) * spread]
        y_real = y[:half, :size]
        y_imag = y[:half, size:]
        row = lax.broadcasted_iota(jnp.int32, y_imag.shape, 0)
        y_imag = jnp.where(row == 0, y[half : half + 1, :size], y_imag)
        both = jnp.concatenate([y_real, y_imag], axis=0).astype(jnp.bfloat16)
        result = product(last, both)
        corr[k] = result
        surface[k] = result.astype(jnp.bfloat16)
    copy.wait()
    lane = lax.broadcasted_iota(jnp.int32, (1, size), 1)
    diagonal = lax.broadcasted_iota(jnp.int32, (cand, cand), 0) == lax.broadcasted_iota(jnp.int32, (cand, cand), 1)
    for k in range(count):
        picked = []
        for j in range(cand):
            row = corr[k, pl.ds(peaks[k, 0, j], 1), :]
            picked.append(jnp.where(lane == peaks[k, 1, j], row, 0.0))
        found = jnp.sum(jnp.concatenate(picked, axis=0), axis=1, keepdims=True)
        scores[k : k + 1, :] = jnp.sum(jnp.where(diagonal, found, 0.0), axis=0, keepdims=True)


def choose_kernel(first, second, out):
    place = lax.axis_index("tile") % PLANE
    outer = (place == 0) | (place == PLANE - 1)

    @pl.when(outer)
    def _():
        out[...] = first[...]

    @pl.when(jnp.logical_not(outer))
    def _():
        out[...] = second[...]


def routes(devices):
    def up(t, c):
        return (t + PLANE, c) if t + PLANE < devices else (t, 1 - c)

    def down(t, c):
        return (t - PLANE, c) if t >= PLANE else (t, 1 - c)

    def across(c, core):
        return 2 if c == core else 1

    def pairs(step):
        return [(2 * t + c, 2 * d + e) for t in range(devices) for c in range(2) for d, e in [step(t, c)]]

    return (
        pairs(lambda t, c: (t ^ across(c, 0), c)),
        pairs(lambda t, c: (t ^ across(c, 1), c)),
        pairs(lambda t, c: (up if (t % PLANE < 2) == (c == 0) else down)(t, c)),
        pairs(lambda t, c: (t ^ across(c, 1), c)),
        pairs(lambda t, c: (up if (t % PLANE < 2) == (c == 1) else down)(t, c)),
    )


def after(value, *earlier):
    return lax.optimization_barrier((value, *earlier))[0]


def call(kernel, name, operands, out, scratch=(), first=VMEM, flops=1 << 30):
    return pl.pallas_call(
        kernel,
        out_shape=out,
        in_specs=[first] + [VMEM] * (len(operands) - 1),
        out_specs=jax.tree.map(lambda _: VMEM, out),
        scratch_shapes=scratch,
        compiler_params=pltpu.CompilerParams(vmem_limit_bytes=8 << 20),
        cost_estimate=pl.CostEstimate(flops=flops, bytes_accessed=1 << 20, transcendentals=0),
        name=name,
    )(*operands)


def spectra_calls(table, slab, name, core, *panels):
    count, size = sum(p.shape[0] for p in panels), panels[0].shape[-1]
    return call(
        functools.partial(spectra_kernel, core),
        "spectra_" + name,
        (*panels, table),
        jax.ShapeDtypeStruct((count, slab, size), jnp.float32),
        flops=count * 12 * size**3,
    )


def chosen(first, second):
    return call(choose_kernel, "choose", (first, second), jax.ShapeDtypeStruct(first.shape, first.dtype), flops=1 << 20)


def shards(panels, pair_ends, peaks):
    tile_dev, _, size, _ = panels.shape
    share, cand, _ = peaks.shape
    devices = lax.axis_size("tile")
    local = panels[:, 0]
    forward, backward = tables(size)
    slab = size + 2 * EXTRA
    swap, cross_swap, climb, relay, climb_late = routes(devices)
    move = functools.partial(lax.ppermute, axis_name=BOTH)
    ends = pair_ends.T
    spots = jnp.transpose(peaks, (0, 2, 1))
    half = tile_dev // 2

    spectra = functools.partial(spectra_calls, forward, slab)
    parts = (local[:half], local[half:])
    got_swap = [move(part, perm=swap) for part in parts]
    own = spectra("own", None, *parts)
    got_cross = [move(after(part, got_swap[0]), perm=cross_swap) for part in parts]
    got_climb = [move(part, perm=climb) for part in got_swap]
    got_relay = [move(chosen(a, b), perm=relay) for a, b in zip(got_swap, got_climb)]
    got_late = [move(part, perm=climb_late) for part in got_cross]
    blocks = [
        own,
        spectra("swap", None, *got_swap),
        spectra("cross", None, *got_cross),
        spectra("climb", 0, *got_climb),
        spectra("late", 1, *got_late),
        spectra("relay", None, got_relay[0]),
    ]
    cuts = [(index, 0) for index in range(len(blocks))] + [(len(blocks) - 1, half)]
    crosses = jax.ShapeDtypeStruct((share, slab, size), jnp.bfloat16)
    taken = pltpu.VMEM((share, slab, size), jnp.float32)
    given, last = call(
        functools.partial(cross_other_kernel, cuts),
        "cross_other",
        (ends, *blocks, got_relay[1], forward),
        (crosses, jax.ShapeDtypeStruct((tile_dev - half, slab, size), jnp.float32)),
        [taken, pltpu.SMEM(ends.shape, ends.dtype), pltpu.SemaphoreType.DMA(())],
        ANY,
        flops=1 << 29,
    )
    other = lax.ppermute(given, "chan", [(0, 1), (1, 0)])
    kept = call(
        functools.partial(cross_mine_kernel, cuts),
        "cross_mine",
        (ends, *blocks, last),
        crosses,
        [taken],
        SMEM,
        flops=1 << 25,
    )
    return call(
        surface_kernel,
        "surface",
        (spots, kept, other, backward),
        (jax.ShapeDtypeStruct((share, size, size), jnp.bfloat16), jax.ShapeDtypeStruct((share, cand), jnp.float32)),
        [pltpu.VMEM((share, size, size), jnp.float32), pltpu.SMEM(spots.shape, spots.dtype), pltpu.SemaphoreType.DMA(())],
        ANY,
    )


def solution(mesh):
    in_specs = (P("tile", "chan", None, None), P("tile", None), P(BOTH, None, None))
    out_specs = (P(BOTH, None, None), P(BOTH, None))
    return jax.shard_map(shards, mesh=mesh, in_specs=in_specs, out_specs=out_specs, check_vma=False)
```

```python
import functools
import math

import jax
import jax.numpy as jnp
import ml_dtypes
import numpy as np
from jax import lax
from jax.experimental import pallas as pl
from jax.experimental.pallas import tpu as pltpu
from jax.sharding import PartitionSpec as P

SIGMA = 0.5
FLOOR = 0.05
PLANE = 4
EXTRA = 8
BOTH = ("tile", "chan")
VMEM = pl.BlockSpec(memory_space=pltpu.VMEM)
SMEM = pl.BlockSpec(memory_space=pltpu.SMEM)
ANY = pl.BlockSpec(memory_space=pl.ANY)


def tables(size):
    index = np.arange(size)
    angle = (index[:, None] * index[None, :] % size) * (2.0 * math.pi / size)
    cosine = np.cos(angle).astype(ml_dtypes.bfloat16).astype(np.float64)
    sine = np.sin(angle).astype(ml_dtypes.bfloat16).astype(np.float64)
    offset = index[:, None] - index[None, :]
    weight = np.exp(-offset * offset / (2.0 * SIGMA * SIGMA))
    gauss = weight / weight.sum(axis=1, keepdims=True)
    half = size // 2
    columns = np.concatenate([cosine, -sine], axis=1)
    pad = np.zeros((EXTRA - 1, 2 * size))
    real = np.concatenate([cosine, sine], axis=1) / size
    imag = np.concatenate([-sine, cosine], axis=1) / size
    rows = np.concatenate([real[:half], imag[:half], real[half : half + 1], pad, imag[half : half + 1], pad], axis=0)
    back = np.block([[cosine, sine], [-sine, cosine]])
    twice = np.full((1, half), 2.0)
    twice[0, 0] = 1.0
    sines = -sine[:, :half] * twice
    sines[:, 0] = cosine[:, half]
    last = np.concatenate([cosine[:, :half] * twice, sines], axis=1) / size
    wide = np.concatenate([gauss.T, gauss], axis=1)
    narrow = np.concatenate([last, np.zeros((size, size))], axis=1)
    forward = np.concatenate([wide, columns, rows], axis=0)
    backward = np.concatenate([back, narrow], axis=0)
    return jnp.asarray(forward.astype(ml_dtypes.bfloat16)), jnp.asarray(backward.astype(ml_dtypes.bfloat16))


def product(left, right):
    return jnp.dot(left, right, preferred_element_type=jnp.float32)


def spectra_of(panels, table):
    count, size, _ = panels.shape
    first = product(panels.reshape(count * size, size), table[:size, :size]).astype(jnp.bfloat16)
    gauss = table[:size, size:]
    smooth = [product(gauss, first[k * size : (k + 1) * size]).astype(jnp.bfloat16) for k in range(count)]
    part = product(jnp.concatenate(smooth, axis=0), table[size : 2 * size]).astype(jnp.bfloat16)
    rows = table[2 * size :]
    slabs = []
    for k in range(count):
        one = part[k * size : (k + 1) * size]
        slabs.append(product(rows, jnp.concatenate([one[:, :size], one[:, size:]], axis=0)))
    return slabs


def spectra_kernel(core, *refs):
    panels, (table, out) = refs[:-2], refs[-2:]

    def work():
        for k, slab in enumerate(spectra_of(jnp.concatenate([p[...] for p in panels], axis=0), table)):
            out[k] = slab

    if core is None:
        work()
    else:
        pl.when(lax.axis_index("chan") == core)(work)


def split(slab, half):
    return (slab[:half], slab[half : 2 * half], slab[2 * half : 2 * half + EXTRA], slab[2 * half + EXTRA :])


def distances(here, chan):
    place = here % PLANE
    one = jnp.where(place % 2 == 0, 1, -1)
    two = jnp.where(place < 2, 2, -2)
    even = chan == 0
    never = 2 * PLANE
    return (
        0,
        jnp.where(even, two, one),
        jnp.where(even, one, two),
        jnp.where(even, -two, never),
        jnp.where(even, never, -two),
        -one,
    )


def cross_slab(a_slab, b_slab, half):
    a_real, a_imag, a_real_x, a_imag_x = split(a_slab, half)
    b_real, b_imag, b_real_x, b_imag_x = split(b_slab, half)
    parts = [
        a_real * b_real + a_imag * b_imag,
        a_imag * b_real - a_real * b_imag,
        a_real_x * b_real_x + a_imag_x * b_imag_x,
        a_imag_x * b_real_x - a_real_x * b_imag_x,
    ]
    return jnp.concatenate(parts, axis=0).astype(jnp.bfloat16)


def write_crosses(first_pair, cuts, ends, blocks, out, taken):
    here = lax.axis_index("tile")
    held = distances(here, lax.axis_index("chan"))
    own = blocks[0]
    tile_dev = own.shape[0]
    half = taken.shape[-1] // 2
    count = out.shape[0]
    for k in range(count):
        tile = ends[1, first_pair + k]
        away = tile // tile_dev - here
        slot = tile % tile_dev
        for (index, base), source in zip(cuts, blocks):
            size = source.shape[0]
            pick = away == held[index]
            if size < tile_dev:
                pick = pick & (slot >= base) & (slot < base + size)

            @pl.when(pick)
            def _(source=source, base=base):
                taken[k] = source[slot - base]

    for k in range(count):
        out[k] = cross_slab(own[ends[0, first_pair + k] - here * tile_dev], taken[k], half)


def cross_other_kernel(cuts, ends, *refs):
    blocks, (panels, table, out, slabs, taken, numbers, sem) = refs[: len(cuts) - 1], refs[len(cuts) - 1 :]
    copy = pltpu.make_async_copy(ends, numbers, sem)
    copy.start()
    for k, slab in enumerate(spectra_of(panels[...], table)):
        slabs[k] = slab
    copy.wait()
    first_pair = out.shape[0] * (1 - lax.axis_index("chan"))
    write_crosses(first_pair, cuts, numbers, (*blocks, slabs), out, taken)


def cross_mine_kernel(cuts, ends, *refs):
    blocks, (out, taken) = refs[: len(cuts)], refs[len(cuts) :]
    write_crosses(out.shape[0] * lax.axis_index("chan"), cuts, ends, blocks, out, taken)


def surface_kernel(spots, mine, other, table, surface, scores, corr, peaks, sem):
    copy = pltpu.make_async_copy(spots, peaks, sem)
    copy.start()
    count, _, size = surface.shape
    cand = scores.shape[1]
    half = size // 2
    parts = []
    for k in range(count):
        slab = mine[k].astype(jnp.float32) + other[k].astype(jnp.float32)
        real, imag, real_x, imag_x = split(slab, half)
        magnitude = jnp.sqrt(real * real + imag * imag)
        magnitude_x = jnp.sqrt(real_x * real_x + imag_x * imag_x)
        total = 2.0 * jnp.sum(magnitude) - jnp.sum(magnitude[:1]) + jnp.sum(magnitude_x)
        level = total / (size * size) + 1e-06
        scale = 1.0 / (magnitude + FLOOR * level)
        scale_x = 1.0 / (magnitude_x + FLOOR * level)
        q_real = jnp.concatenate([real * scale, real_x * scale_x], axis=0)
        q_imag = jnp.concatenate([imag * scale, imag_x * scale_x], axis=0)
        parts.append(jnp.concatenate([q_real, q_imag], axis=1))
    spread = half + EXTRA
    y_all = product(jnp.concatenate(parts, axis=0).astype(jnp.bfloat16), table[: 2 * size])
    last = table[2 * size :, :size]
    for k in range(count):
        y = y_all[k * spread : (k + 1) * spread]
        y_real = y[:half, :size]
        y_imag = y[:half, size:]
        row = lax.broadcasted_iota(jnp.int32, y_imag.shape, 0)
        y_imag = jnp.where(row == 0, y[half : half + 1, :size], y_imag)
        both = jnp.concatenate([y_real, y_imag], axis=0).astype(jnp.bfloat16)
        result = product(last, both)
        corr[k] = result
        surface[k] = result.astype(jnp.bfloat16)
    copy.wait()
    lane = lax.broadcasted_iota(jnp.int32, (1, size), 1)
    diagonal = lax.broadcasted_iota(jnp.int32, (cand, cand), 0) == lax.broadcasted_iota(jnp.int32, (cand, cand), 1)
    for k in range(count):
        picked = []
        for j in range(cand):
            row = corr[k, pl.ds(peaks[k, 0, j], 1), :]
            picked.append(jnp.where(lane == peaks[k, 1, j], row, 0.0))
        found = jnp.sum(jnp.concatenate(picked, axis=0), axis=1, keepdims=True)
        scores[k : k + 1, :] = jnp.sum(jnp.where(diagonal, found, 0.0), axis=0, keepdims=True)


def choose_kernel(first, second, out):
    place = lax.axis_index("tile") % PLANE
    outer = (place == 0) | (place == PLANE - 1)

    @pl.when(outer)
    def _():
        out[...] = first[...]

    @pl.when(jnp.logical_not(outer))
    def _():
        out[...] = second[...]


def routes(devices):
    def up(t, c):
        return (t + PLANE, c) if t + PLANE < devices else (t, 1 - c)

    def down(t, c):
        return (t - PLANE, c) if t >= PLANE else (t, 1 - c)

    def across(c, core):
        return 2 if c == core else 1

    def pairs(step):
        return [(2 * t + c, 2 * d + e) for t in range(devices) for c in range(2) for d, e in [step(t, c)]]

    return (
        pairs(lambda t, c: (t ^ across(c, 0), c)),
        pairs(lambda t, c: (t ^ across(c, 1), c)),
        pairs(lambda t, c: (up if (t % PLANE < 2) == (c == 0) else down)(t, c)),
        pairs(lambda t, c: (t ^ across(c, 1), c)),
        pairs(lambda t, c: (up if (t % PLANE < 2) == (c == 1) else down)(t, c)),
    )


def after(value, *earlier):
    return lax.optimization_barrier((value, *earlier))[0]


def call(kernel, name, operands, out, scratch=(), first=VMEM, flops=1 << 30):
    return pl.pallas_call(
        kernel,
        out_shape=out,
        in_specs=[first] + [VMEM] * (len(operands) - 1),
        out_specs=jax.tree.map(lambda _: VMEM, out),
        scratch_shapes=scratch,
        compiler_params=pltpu.CompilerParams(vmem_limit_bytes=8 << 20),
        cost_estimate=pl.CostEstimate(flops=flops, bytes_accessed=1 << 20, transcendentals=0),
        name=name,
    )(*operands)


def spectra_calls(table, slab, name, core, *panels, flops=None):
    count, size = sum(p.shape[0] for p in panels), panels[0].shape[-1]
    return call(
        functools.partial(spectra_kernel, core),
        "spectra_" + name,
        (*panels, table),
        jax.ShapeDtypeStruct((count, slab, size), jnp.float32),
        flops=flops or count * 12 * size**3,
    )


def chosen(first, second, flops):
    return call(choose_kernel, "choose", (first, second), jax.ShapeDtypeStruct(first.shape, first.dtype), flops=flops)


def shards(panels, pair_ends, peaks):
    tile_dev, _, size, _ = panels.shape
    share, cand, _ = peaks.shape
    devices = lax.axis_size("tile")
    local = panels[:, 0]
    forward, backward = tables(size)
    slab = size + 2 * EXTRA
    swap, cross_swap, climb, relay, climb_late = routes(devices)
    move = functools.partial(lax.ppermute, axis_name=BOTH)
    ends = pair_ends.T
    spots = jnp.transpose(peaks, (0, 2, 1))
    half = tile_dev // 2

    spectra = functools.partial(spectra_calls, forward, slab)
    parts = (local[:half], local[half:])
    got_swap = [move(part, perm=swap) for part in parts]
    own = spectra("own", None, *parts)
    got_cross = [move(after(part, got_swap[0], own), perm=cross_swap) for part in parts]
    got_climb = [move(part, perm=climb) for part in got_swap]
    picked = [chosen(a, b, flops) for a, b, flops in zip(got_swap, got_climb, (1 << 20, 3_000_000_000))]
    got_relay = [move(part, perm=relay) for part in picked]
    got_late = [move(part, perm=climb_late) for part in got_cross]
    from_swap = spectra("swap", None, after(got_swap[0], got_relay[0]), got_swap[1])
    from_cross = spectra("cross", None, *got_cross, flops=1_000_000)
    from_climb = spectra("climb", 0, after(got_climb[0], from_swap), got_climb[1], flops=1_000_000)
    from_relay = spectra("relay", None, got_relay[0], flops=800_000_000)
    from_late = spectra("late", 1, *got_late)
    blocks = [own, from_swap, from_cross, from_climb, from_late, from_relay]
    cuts = [(index, 0) for index in range(len(blocks))] + [(len(blocks) - 1, half)]
    crosses = jax.ShapeDtypeStruct((share, slab, size), jnp.bfloat16)
    taken = pltpu.VMEM((share, slab, size), jnp.float32)
    given, last = call(
        functools.partial(cross_other_kernel, cuts),
        "cross_other",
        (ends, *blocks, got_relay[1], forward),
        (crosses, jax.ShapeDtypeStruct((tile_dev - half, slab, size), jnp.float32)),
        [taken, pltpu.SMEM(ends.shape, ends.dtype), pltpu.SemaphoreType.DMA(())],
        ANY,
        flops=1 << 29,
    )
    other = lax.ppermute(given, "chan", [(0, 1), (1, 0)])
    kept = call(
        functools.partial(cross_mine_kernel, cuts),
        "cross_mine",
        (ends, *blocks, last),
        crosses,
        [taken],
        SMEM,
        flops=1 << 25,
    )
    return call(
        surface_kernel,
        "surface",
        (spots, kept, other, backward),
        (jax.ShapeDtypeStruct((share, size, size), jnp.bfloat16), jax.ShapeDtypeStruct((share, cand), jnp.float32)),
        [pltpu.VMEM((share, size, size), jnp.float32), pltpu.SMEM(spots.shape, spots.dtype), pltpu.SemaphoreType.DMA(())],
        ANY,
    )


def solution(mesh):
    in_specs = (P("tile", "chan", None, None), P("tile", None), P(BOTH, None, None))
    out_specs = (P(BOTH, None, None), P(BOTH, None))
    return jax.shard_map(shards, mesh=mesh, in_specs=in_specs, out_specs=out_specs, check_vma=False)
```

```python
import functools
import math

import jax
import jax.numpy as jnp
import ml_dtypes
import numpy as np
from jax import lax
from jax.experimental import pallas as pl
from jax.experimental.pallas import tpu as pltpu
from jax.sharding import PartitionSpec as P

SIGMA = 0.5
FLOOR = 0.05
PLANE = 4
EXTRA = 8
BOTH = ("tile", "chan")
VMEM = pl.BlockSpec(memory_space=pltpu.VMEM)
SMEM = pl.BlockSpec(memory_space=pltpu.SMEM)
ANY = pl.BlockSpec(memory_space=pl.ANY)


def tables(size):
    index = np.arange(size)
    angle = (index[:, None] * index[None, :] % size) * (2.0 * math.pi / size)
    cosine = np.cos(angle).astype(ml_dtypes.bfloat16).astype(np.float64)
    sine = np.sin(angle).astype(ml_dtypes.bfloat16).astype(np.float64)
    offset = index[:, None] - index[None, :]
    weight = np.exp(-offset * offset / (2.0 * SIGMA * SIGMA))
    gauss = weight / weight.sum(axis=1, keepdims=True)
    half = size // 2
    columns = np.concatenate([cosine, -sine], axis=1)
    pad = np.zeros((EXTRA - 1, 2 * size))
    real = np.concatenate([cosine, sine], axis=1) / size
    imag = np.concatenate([-sine, cosine], axis=1) / size
    rows = np.concatenate([real[:half], imag[:half], real[half : half + 1], pad, imag[half : half + 1], pad], axis=0)
    back = np.block([[cosine, sine], [-sine, cosine]])
    twice = np.full((1, half), 2.0)
    twice[0, 0] = 1.0
    sines = -sine[:, :half] * twice
    sines[:, 0] = cosine[:, half]
    last = np.concatenate([cosine[:, :half] * twice, sines], axis=1) / size
    wide = np.concatenate([gauss.T, gauss], axis=1)
    narrow = np.concatenate([last, np.zeros((size, size))], axis=1)
    forward = np.concatenate([wide, columns, rows], axis=0)
    backward = np.concatenate([back, narrow], axis=0)
    return jnp.asarray(forward.astype(ml_dtypes.bfloat16)), jnp.asarray(backward.astype(ml_dtypes.bfloat16))


def product(left, right):
    return jnp.dot(left, right, preferred_element_type=jnp.float32)


def spectra_of(panels, table):
    count, size, _ = panels.shape
    first = product(panels.reshape(count * size, size), table[:size, :size]).astype(jnp.bfloat16)
    gauss = table[:size, size:]
    smooth = [product(gauss, first[k * size : (k + 1) * size]).astype(jnp.bfloat16) for k in range(count)]
    part = product(jnp.concatenate(smooth, axis=0), table[size : 2 * size]).astype(jnp.bfloat16)
    rows = table[2 * size :]
    slabs = []
    for k in range(count):
        one = part[k * size : (k + 1) * size]
        slabs.append(product(rows, jnp.concatenate([one[:, :size], one[:, size:]], axis=0)))
    return slabs


def spectra_kernel(core, *refs):
    panels, (table, out) = refs[:-2], refs[-2:]

    def work():
        for k, slab in enumerate(spectra_of(jnp.concatenate([p[...] for p in panels], axis=0), table)):
            out[k] = slab

    if core is None:
        work()
    else:
        pl.when(lax.axis_index("chan") == core)(work)


def split(slab, half):
    return (slab[:half], slab[half : 2 * half], slab[2 * half : 2 * half + EXTRA], slab[2 * half + EXTRA :])


def distances(here, chan):
    place = here % PLANE
    one = jnp.where(place % 2 == 0, 1, -1)
    two = jnp.where(place < 2, 2, -2)
    even = chan == 0
    never = 2 * PLANE
    return (
        0,
        jnp.where(even, two, one),
        jnp.where(even, one, two),
        jnp.where(even, -two, never),
        jnp.where(even, never, -two),
        -one,
    )


def cross_slab(a_slab, b_slab, half):
    a_real, a_imag, a_real_x, a_imag_x = split(a_slab, half)
    b_real, b_imag, b_real_x, b_imag_x = split(b_slab, half)
    parts = [
        a_real * b_real + a_imag * b_imag,
        a_imag * b_real - a_real * b_imag,
        a_real_x * b_real_x + a_imag_x * b_imag_x,
        a_imag_x * b_real_x - a_real_x * b_imag_x,
    ]
    return jnp.concatenate(parts, axis=0).astype(jnp.bfloat16)


def write_crosses(first_pair, cuts, ends, blocks, out):
    here = lax.axis_index("tile")
    held = distances(here, lax.axis_index("chan"))
    own = blocks[0]
    tile_dev = own.shape[0]
    half = out.shape[-1] // 2

    for k in range(out.shape[0]):
        pair = first_pair + k
        tile = ends[1, pair]
        away = tile // tile_dev - here
        slot = tile % tile_dev
        mine = ends[0, pair] - here * tile_dev
        for (index, base), source in zip(cuts, blocks):
            size = source.shape[0]
            pick = away == held[index]
            if size < tile_dev:
                pick = pick & (slot >= base) & (slot < base + size)

            @pl.when(pick)
            def _(source=source, base=base):
                out[k] = cross_slab(own[mine], source[slot - base], half)


def cross_other_kernel(cuts, ends, *refs):
    blocks, (panels, table, out, slabs, numbers, sem) = refs[: len(cuts) - 1], refs[len(cuts) - 1 :]
    copy = pltpu.make_async_copy(ends, numbers, sem)
    copy.start()
    for k, slab in enumerate(spectra_of(panels[...], table)):
        slabs[k] = slab
    copy.wait()
    first_pair = out.shape[0] * (1 - lax.axis_index("chan"))
    write_crosses(first_pair, cuts, numbers, (*blocks, slabs), out)


def cross_mine_kernel(cuts, ends, *refs):
    blocks, out = refs[: len(cuts)], refs[len(cuts)]
    write_crosses(out.shape[0] * lax.axis_index("chan"), cuts, ends, blocks, out)


def quotient(slab, half):
    real, imag, real_x, imag_x = split(slab, half)
    magnitude = jnp.sqrt(real * real + imag * imag)
    magnitude_x = jnp.sqrt(real_x * real_x + imag_x * imag_x)
    columns = 2.0 * jnp.sum(magnitude, axis=0, keepdims=True) - magnitude[:1]
    columns = columns + jnp.sum(magnitude_x, axis=0, keepdims=True)
    level = jnp.sum(columns, axis=1, keepdims=True) / (4 * half * half) + 1e-06
    scale = 1.0 / (magnitude + FLOOR * level)
    scale_x = 1.0 / (magnitude_x + FLOOR * level)
    q_real = jnp.concatenate([real * scale, real_x * scale_x], axis=0)
    q_imag = jnp.concatenate([imag * scale, imag_x * scale_x], axis=0)
    return jnp.concatenate([q_real, q_imag], axis=1)


def surface_kernel(spots, mine, other, table, surface, scores, corr, rounded, found, peaks, sem, sems):
    fetch = pltpu.make_async_copy(spots, peaks, sem)
    fetch.start()
    count, _, size = surface.shape
    cand = scores.shape[1]
    half = size // 2
    parts = [quotient(mine[k].astype(jnp.float32) + other[k].astype(jnp.float32), half) for k in range(count)]
    spread = half + EXTRA
    y_all = product(jnp.concatenate(parts, axis=0).astype(jnp.bfloat16), table[: 2 * size])
    last = table[2 * size :, :size]
    copies = []
    for k in range(count):
        y = y_all[k * spread : (k + 1) * spread]
        y_real = y[:half, :size]
        y_imag = y[:half, size:]
        row = lax.broadcasted_iota(jnp.int32, y_imag.shape, 0)
        y_imag = jnp.where(row == 0, y[half : half + 1, :size], y_imag)
        both = jnp.concatenate([y_real, y_imag], axis=0).astype(jnp.bfloat16)
        result = product(last, both)
        corr[k] = result
        rounded[k] = result.astype(jnp.bfloat16)
        copies.append(pltpu.make_async_copy(rounded.at[k], surface.at[k], sems.at[k]))
        copies[-1].start()
    fetch.wait()
    lane = lax.broadcasted_iota(jnp.int32, (1, size), 1)
    diagonal = lax.broadcasted_iota(jnp.int32, (cand, cand), 0) == lax.broadcasted_iota(jnp.int32, (cand, cand), 1)
    for k in range(count):
        picked = []
        for j in range(cand):
            row = corr[k, pl.ds(peaks[k, 0, j], 1), :]
            picked.append(jnp.where(lane == peaks[k, 1, j], row, 0.0))
        sums = jnp.sum(jnp.concatenate(picked, axis=0), axis=1, keepdims=True)
        found[k : k + 1, :] = jnp.sum(jnp.where(diagonal, sums, 0.0), axis=0, keepdims=True)
    copies.append(pltpu.make_async_copy(found, scores, sems.at[count]))
    copies[-1].start()
    for copy in copies:
        copy.wait()


def choose_kernel(first, second, out):
    place = lax.axis_index("tile") % PLANE
    outer = (place == 0) | (place == PLANE - 1)

    @pl.when(outer)
    def _():
        out[...] = first[...]

    @pl.when(jnp.logical_not(outer))
    def _():
        out[...] = second[...]


def routes(devices):
    def up(t, c):
        return (t + PLANE, c) if t + PLANE < devices else (t, 1 - c)

    def down(t, c):
        return (t - PLANE, c) if t >= PLANE else (t, 1 - c)

    def across(c, core):
        return 2 if c == core else 1

    def pairs(step):
        return [(2 * t + c, 2 * d + e) for t in range(devices) for c in range(2) for d, e in [step(t, c)]]

    return (
        pairs(lambda t, c: (t ^ across(c, 0), c)),
        pairs(lambda t, c: (t ^ across(c, 1), c)),
        pairs(lambda t, c: (up if (t % PLANE < 2) == (c == 0) else down)(t, c)),
        pairs(lambda t, c: (t ^ across(c, 1), c)),
        pairs(lambda t, c: (up if (t % PLANE < 2) == (c == 1) else down)(t, c)),
    )


def after(value, *earlier):
    return lax.optimization_barrier((value, *earlier))[0]


def call(kernel, name, operands, out, scratch=(), first=VMEM, flops=1 << 30, results=VMEM):
    return pl.pallas_call(
        kernel,
        out_shape=out,
        in_specs=[first] + [VMEM] * (len(operands) - 1),
        out_specs=jax.tree.map(lambda _: results, out),
        scratch_shapes=scratch,
        compiler_params=pltpu.CompilerParams(vmem_limit_bytes=8 << 20),
        cost_estimate=pl.CostEstimate(flops=flops, bytes_accessed=1 << 20, transcendentals=0),
        name=name,
    )(*operands)


def spectra_calls(table, slab, name, core, *panels, flops=None):
    count, size = sum(p.shape[0] for p in panels), panels[0].shape[-1]
    return call(
        functools.partial(spectra_kernel, core),
        "spectra_" + name,
        (*panels, table),
        jax.ShapeDtypeStruct((count, slab, size), jnp.float32),
        flops=flops or count * 12 * size**3,
    )


def chosen(first, second, flops):
    return call(choose_kernel, "choose", (first, second), jax.ShapeDtypeStruct(first.shape, first.dtype), flops=flops)


def shards(panels, pair_ends, peaks):
    tile_dev, _, size, _ = panels.shape
    share, cand, _ = peaks.shape
    devices = lax.axis_size("tile")
    local = panels[:, 0]
    forward, backward = tables(size)
    slab = size + 2 * EXTRA
    swap, cross_swap, climb, relay, climb_late = routes(devices)
    move = functools.partial(lax.ppermute, axis_name=BOTH)
    ends = pair_ends.T
    spots = jnp.transpose(peaks, (0, 2, 1))
    half = tile_dev // 2

    spectra = functools.partial(spectra_calls, forward, slab)
    parts = (local[:half], local[half:])
    got_swap = [move(part, perm=swap) for part in parts]
    own = spectra("own", None, *parts)
    got_cross = [move(after(part, got_swap[0], own), perm=cross_swap) for part in parts]
    got_climb = [move(part, perm=climb) for part in got_swap]
    picked = [chosen(a, b, flops) for a, b, flops in zip(got_swap, got_climb, (1 << 20, 3_000_000_000))]
    got_relay = [move(part, perm=relay) for part in picked]
    got_late = [move(part, perm=climb_late) for part in got_cross]
    from_swap = spectra("swap", None, after(got_swap[0], got_relay[0]), got_swap[1])
    from_cross = spectra("cross", None, *got_cross, flops=1_000_000)
    from_climb = spectra("climb", 0, after(got_climb[0], from_swap), got_climb[1], flops=1_000_000)
    from_relay = spectra("relay", None, got_relay[0], flops=800_000_000)
    from_late = spectra("late", 1, *got_late)
    blocks = [own, from_swap, from_cross, from_climb, from_late, from_relay]
    cuts = [(index, 0) for index in range(len(blocks))] + [(len(blocks) - 1, half)]
    crosses = jax.ShapeDtypeStruct((share, slab, size), jnp.bfloat16)
    given, last = call(
        functools.partial(cross_other_kernel, cuts),
        "cross_other",
        (ends, *blocks, got_relay[1], forward),
        (crosses, jax.ShapeDtypeStruct((tile_dev - half, slab, size), jnp.float32)),
        [pltpu.SMEM(ends.shape, ends.dtype), pltpu.SemaphoreType.DMA(())],
        ANY,
        flops=1 << 29,
    )
    other = lax.ppermute(given, "chan", [(0, 1), (1, 0)])
    kept = call(
        functools.partial(cross_mine_kernel, cuts),
        "cross_mine",
        (ends, *blocks, last),
        crosses,
        first=SMEM,
        flops=1 << 25,
    )
    return call(
        surface_kernel,
        "surface",
        (spots, kept, other, backward),
        (jax.ShapeDtypeStruct((share, size, size), jnp.bfloat16), jax.ShapeDtypeStruct((share, cand), jnp.float32)),
        [
            pltpu.VMEM((share, size, size), jnp.float32),
            pltpu.VMEM((share, size, size), jnp.bfloat16),
            pltpu.VMEM((share, cand), jnp.float32),
            pltpu.SMEM(spots.shape, spots.dtype),
            pltpu.SemaphoreType.DMA(()),
            pltpu.SemaphoreType.DMA((share + 1,)),
        ],
        ANY,
        results=ANY,
    )


def solution(mesh):
    in_specs = (P("tile", "chan", None, None), P("tile", None), P(BOTH, None, None))
    out_specs = (P(BOTH, None, None), P(BOTH, None))
    return jax.shard_map(shards, mesh=mesh, in_specs=in_specs, out_specs=out_specs, check_vma=False)
```

```python
import functools
import math

import jax
import jax.numpy as jnp
import ml_dtypes
import numpy as np
from jax import lax
from jax.experimental import pallas as pl
from jax.experimental.pallas import tpu as pltpu
from jax.sharding import PartitionSpec as P

SIGMA = 0.5
FLOOR = 0.05
PLANE = 4
EXTRA = 8
BOTH = ("tile", "chan")
VMEM = pl.BlockSpec(memory_space=pltpu.VMEM)
SMEM = pl.BlockSpec(memory_space=pltpu.SMEM)
ANY = pl.BlockSpec(memory_space=pl.ANY)


def tables(size):
    index = np.arange(size)
    angle = (index[:, None] * index[None, :] % size) * (2.0 * math.pi / size)
    cosine = np.cos(angle).astype(ml_dtypes.bfloat16).astype(np.float64)
    sine = np.sin(angle).astype(ml_dtypes.bfloat16).astype(np.float64)
    offset = index[:, None] - index[None, :]
    weight = np.exp(-offset * offset / (2.0 * SIGMA * SIGMA))
    gauss = weight / weight.sum(axis=1, keepdims=True)
    half = size // 2
    columns = np.concatenate([cosine, -sine], axis=1)
    pad = np.zeros((EXTRA - 1, 2 * size))
    real = np.concatenate([cosine, sine], axis=1) / size
    imag = np.concatenate([-sine, cosine], axis=1) / size
    rows = np.concatenate([real[:half], imag[:half], real[half : half + 1], pad, imag[half : half + 1], pad], axis=0)
    back = np.block([[cosine, sine], [-sine, cosine]])
    twice = np.full((1, half), 2.0)
    twice[0, 0] = 1.0
    sines = -sine[:, :half] * twice
    sines[:, 0] = cosine[:, half]
    last = np.concatenate([cosine[:, :half] * twice, sines], axis=1) / size
    wide = np.concatenate([gauss.T, gauss], axis=1)
    narrow = np.concatenate([last, np.zeros((size, size))], axis=1)
    forward = np.concatenate([wide, columns, rows], axis=0)
    backward = np.concatenate([back, narrow], axis=0)
    return jnp.asarray(forward.astype(ml_dtypes.bfloat16)), jnp.asarray(backward.astype(ml_dtypes.bfloat16))


def product(left, right):
    return jnp.dot(left, right, preferred_element_type=jnp.float32)


def spectra_of(panels, table):
    count, size, _ = panels.shape
    right = table[:size, :size]
    if count > 2:
        first = [product(panels[k], right).astype(jnp.bfloat16) for k in range(count)]
    else:
        stack = product(panels.reshape(count * size, size), right).astype(jnp.bfloat16)
        first = [stack[k * size : (k + 1) * size] for k in range(count)]
    gauss = table[:size, size:]
    smooth = [product(gauss, one).astype(jnp.bfloat16) for one in first]
    if count > 2:
        parts = [product(one, table[size : 2 * size]).astype(jnp.bfloat16) for one in smooth]
    else:
        stack = product(jnp.concatenate(smooth, axis=0), table[size : 2 * size]).astype(jnp.bfloat16)
        parts = [stack[k * size : (k + 1) * size] for k in range(count)]
    rows = table[2 * size :]
    return [product(rows, jnp.concatenate([one[:, :size], one[:, size:]], axis=0)) for one in parts]


def spectra_kernel(core, *refs):
    panels, (table, out) = refs[:-2], refs[-2:]

    def work():
        for k, slab in enumerate(spectra_of(jnp.concatenate([p[...] for p in panels], axis=0), table)):
            out[k] = slab

    if core is None:
        work()
    else:
        pl.when(lax.axis_index("chan") == core)(work)


def split(slab, half):
    return (slab[:half], slab[half : 2 * half], slab[2 * half : 2 * half + EXTRA], slab[2 * half + EXTRA :])


def distances(here, chan):
    place = here % PLANE
    one = jnp.where(place % 2 == 0, 1, -1)
    two = jnp.where(place < 2, 2, -2)
    even = chan == 0
    never = 2 * PLANE
    return (
        0,
        jnp.where(even, two, one),
        jnp.where(even, one, two),
        jnp.where(even, -two, never),
        jnp.where(even, never, -two),
        -one,
    )


def cross_slab(a_slab, b_slab, half):
    a_real, a_imag, a_real_x, a_imag_x = split(a_slab, half)
    b_real, b_imag, b_real_x, b_imag_x = split(b_slab, half)
    parts = [
        a_real * b_real + a_imag * b_imag,
        a_imag * b_real - a_real * b_imag,
        a_real_x * b_real_x + a_imag_x * b_imag_x,
        a_imag_x * b_real_x - a_real_x * b_imag_x,
    ]
    return jnp.concatenate(parts, axis=0).astype(jnp.bfloat16)


def write_crosses(first_pair, cuts, ends, blocks, out):
    here = lax.axis_index("tile")
    held = distances(here, lax.axis_index("chan"))
    own = blocks[0]
    tile_dev = own.shape[0]
    half = out.shape[-1] // 2

    for k in range(out.shape[0]):
        pair = first_pair + k
        tile = ends[1, pair]
        away = tile // tile_dev - here
        slot = tile % tile_dev
        mine = ends[0, pair] - here * tile_dev
        for (index, base), source in zip(cuts, blocks):
            size = source.shape[0]
            pick = away == held[index]
            if size < tile_dev:
                pick = pick & (slot >= base) & (slot < base + size)

            @pl.when(pick)
            def _(source=source, base=base):
                out[k] = cross_slab(own[mine], source[slot - base], half)


def cross_other_kernel(cuts, ends, *refs):
    blocks, (panels, table, out, slabs, numbers, sem) = refs[: len(cuts) - 1], refs[len(cuts) - 1 :]
    copy = pltpu.make_async_copy(ends, numbers, sem)
    copy.start()
    for k, slab in enumerate(spectra_of(panels[...], table)):
        slabs[k] = slab
    copy.wait()
    first_pair = out.shape[0] * (1 - lax.axis_index("chan"))
    write_crosses(first_pair, cuts, numbers, (*blocks, slabs), out)


def cross_mine_kernel(cuts, ends, *refs):
    blocks, out = refs[: len(cuts)], refs[len(cuts)]
    write_crosses(out.shape[0] * lax.axis_index("chan"), cuts, ends, blocks, out)


def quotient(slab, half):
    real, imag, real_x, imag_x = split(slab, half)
    magnitude = jnp.sqrt(real * real + imag * imag)
    magnitude_x = jnp.sqrt(real_x * real_x + imag_x * imag_x)
    columns = 2.0 * jnp.sum(magnitude, axis=0, keepdims=True) - magnitude[:1]
    columns = columns + jnp.sum(magnitude_x, axis=0, keepdims=True)
    level = jnp.sum(columns, axis=1, keepdims=True) / (4 * half * half) + 1e-06
    scale = 1.0 / (magnitude + FLOOR * level)
    scale_x = 1.0 / (magnitude_x + FLOOR * level)
    q_real = jnp.concatenate([real * scale, real_x * scale_x], axis=0)
    q_imag = jnp.concatenate([imag * scale, imag_x * scale_x], axis=0)
    return jnp.concatenate([q_real, q_imag], axis=1)


def surface_kernel(spots, mine, other, table, surface, scores, corr, rounded, found, peaks, sem, sems):
    fetch = pltpu.make_async_copy(spots, peaks, sem)
    fetch.start()
    count, _, size = surface.shape
    cand = scores.shape[1]
    half = size // 2
    parts = [quotient(mine[k].astype(jnp.float32) + other[k].astype(jnp.float32), half) for k in range(count)]
    spread = half + EXTRA
    y_all = product(jnp.concatenate(parts, axis=0).astype(jnp.bfloat16), table[: 2 * size])
    last = table[2 * size :, :size]
    copies = []
    for k in range(count):
        y = y_all[k * spread : (k + 1) * spread]
        y_real = y[:half, :size]
        y_imag = y[:half, size:]
        row = lax.broadcasted_iota(jnp.int32, y_imag.shape, 0)
        y_imag = jnp.where(row == 0, y[half : half + 1, :size], y_imag)
        both = jnp.concatenate([y_real, y_imag], axis=0).astype(jnp.bfloat16)
        result = product(last, both)
        corr[k] = result
        rounded[k] = result.astype(jnp.bfloat16)
        copies.append(pltpu.make_async_copy(rounded.at[k], surface.at[k], sems.at[k]))
        copies[-1].start()
    fetch.wait()
    lane = lax.broadcasted_iota(jnp.int32, (1, size), 1)
    diagonal = lax.broadcasted_iota(jnp.int32, (cand, cand), 0) == lax.broadcasted_iota(jnp.int32, (cand, cand), 1)
    for k in range(count):
        picked = []
        for j in range(cand):
            row = corr[k, pl.ds(peaks[k, 0, j], 1), :]
            picked.append(jnp.where(lane == peaks[k, 1, j], row, 0.0))
        sums = jnp.sum(jnp.concatenate(picked, axis=0), axis=1, keepdims=True)
        found[k : k + 1, :] = jnp.sum(jnp.where(diagonal, sums, 0.0), axis=0, keepdims=True)
    copies.append(pltpu.make_async_copy(found, scores, sems.at[count]))
    copies[-1].start()
    for copy in copies:
        copy.wait()


def choose_kernel(first, second, out):
    place = lax.axis_index("tile") % PLANE
    outer = (place == 0) | (place == PLANE - 1)

    @pl.when(outer)
    def _():
        out[...] = first[...]

    @pl.when(jnp.logical_not(outer))
    def _():
        out[...] = second[...]


def routes(devices):
    def up(t, c):
        return (t + PLANE, c) if t + PLANE < devices else (t, 1 - c)

    def down(t, c):
        return (t - PLANE, c) if t >= PLANE else (t, 1 - c)

    def across(c, core):
        return 2 if c == core else 1

    def pairs(step):
        return [(2 * t + c, 2 * d + e) for t in range(devices) for c in range(2) for d, e in [step(t, c)]]

    return (
        pairs(lambda t, c: (t ^ across(c, 0), c)),
        pairs(lambda t, c: (t ^ across(c, 1), c)),
        pairs(lambda t, c: (up if (t % PLANE < 2) == (c == 0) else down)(t, c)),
        pairs(lambda t, c: (t ^ across(c, 1), c)),
        pairs(lambda t, c: (up if (t % PLANE < 2) == (c == 1) else down)(t, c)),
    )


def after(value, *earlier):
    return lax.optimization_barrier((value, *earlier))[0]


def call(kernel, name, operands, out, scratch=(), first=VMEM, flops=1 << 30, results=VMEM):
    return pl.pallas_call(
        kernel,
        out_shape=out,
        in_specs=[first] + [VMEM] * (len(operands) - 1),
        out_specs=jax.tree.map(lambda _: results, out),
        scratch_shapes=scratch,
        compiler_params=pltpu.CompilerParams(vmem_limit_bytes=8 << 20),
        cost_estimate=pl.CostEstimate(flops=flops, bytes_accessed=1 << 20, transcendentals=0),
        name=name,
    )(*operands)


def spectra_calls(table, slab, name, core, *panels, flops=None):
    count, size = sum(p.shape[0] for p in panels), panels[0].shape[-1]
    return call(
        functools.partial(spectra_kernel, core),
        "spectra_" + name,
        (*panels, table),
        jax.ShapeDtypeStruct((count, slab, size), jnp.float32),
        flops=flops or count * 12 * size**3,
    )


def chosen(first, second, flops):
    return call(choose_kernel, "choose", (first, second), jax.ShapeDtypeStruct(first.shape, first.dtype), flops=flops)


def shards(panels, pair_ends, peaks):
    tile_dev, _, size, _ = panels.shape
    share, cand, _ = peaks.shape
    devices = lax.axis_size("tile")
    local = panels[:, 0]
    forward, backward = tables(size)
    slab = size + 2 * EXTRA
    swap, cross_swap, climb, relay, climb_late = routes(devices)
    move = functools.partial(lax.ppermute, axis_name=BOTH)
    ends = pair_ends.T
    spots = jnp.transpose(peaks, (0, 2, 1))
    half = tile_dev // 2

    spectra = functools.partial(spectra_calls, forward, slab)
    parts = (local[:half], local[half:])
    got_swap = [move(part, perm=swap) for part in parts]
    own = spectra("own", None, *parts)
    got_cross = [move(after(part, got_swap[0], own), perm=cross_swap) for part in parts]
    got_climb = [move(part, perm=climb) for part in got_swap]
    picked = [chosen(a, b, flops) for a, b, flops in zip(got_swap, got_climb, (1 << 20, 3_000_000_000))]
    got_relay = [move(part, perm=relay) for part in picked]
    got_late = [move(part, perm=climb_late) for part in got_cross]
    from_swap = spectra("swap", None, after(got_swap[0], got_relay[0]), got_swap[1])
    from_cross = spectra("cross", None, *got_cross, flops=1_000_000)
    from_climb = spectra("climb", 0, after(got_climb[0], from_swap), got_climb[1], flops=1_000_000)
    from_relay = spectra("relay", None, got_relay[0], flops=800_000_000)
    from_late = spectra("late", 1, *got_late)
    blocks = [own, from_swap, from_cross, from_climb, from_late, from_relay]
    cuts = [(index, 0) for index in range(len(blocks))] + [(len(blocks) - 1, half)]
    crosses = jax.ShapeDtypeStruct((share, slab, size), jnp.bfloat16)
    given, last = call(
        functools.partial(cross_other_kernel, cuts),
        "cross_other",
        (ends, *blocks, got_relay[1], forward),
        (crosses, jax.ShapeDtypeStruct((tile_dev - half, slab, size), jnp.float32)),
        [pltpu.SMEM(ends.shape, ends.dtype), pltpu.SemaphoreType.DMA(())],
        ANY,
        flops=1 << 29,
    )
    other = lax.ppermute(given, "chan", [(0, 1), (1, 0)])
    kept = call(
        functools.partial(cross_mine_kernel, cuts),
        "cross_mine",
        (ends, *blocks, last),
        crosses,
        first=SMEM,
        flops=1 << 25,
    )
    return call(
        surface_kernel,
        "surface",
        (spots, kept, other, backward),
        (jax.ShapeDtypeStruct((share, size, size), jnp.bfloat16), jax.ShapeDtypeStruct((share, cand), jnp.float32)),
        [
            pltpu.VMEM((share, size, size), jnp.float32),
            pltpu.VMEM((share, size, size), jnp.bfloat16),
            pltpu.VMEM((share, cand), jnp.float32),
            pltpu.SMEM(spots.shape, spots.dtype),
            pltpu.SemaphoreType.DMA(()),
            pltpu.SemaphoreType.DMA((share + 1,)),
        ],
        ANY,
        results=ANY,
    )


def solution(mesh):
    in_specs = (P("tile", "chan", None, None), P("tile", None), P(BOTH, None, None))
    out_specs = (P(BOTH, None, None), P(BOTH, None))
    return jax.shard_map(shards, mesh=mesh, in_specs=in_specs, out_specs=out_specs, check_vma=False)
```

```python
import functools
import math

import jax
import jax.numpy as jnp
import ml_dtypes
import numpy as np
from jax import lax
from jax.experimental import pallas as pl
from jax.experimental.pallas import tpu as pltpu
from jax.sharding import PartitionSpec as P

SIGMA = 0.5
FLOOR = 0.05
PLANE = 4
EXTRA = 8
BOTH = ("tile", "chan")
VMEM = pl.BlockSpec(memory_space=pltpu.VMEM)
SMEM = pl.BlockSpec(memory_space=pltpu.SMEM)
ANY = pl.BlockSpec(memory_space=pl.ANY)


def tables(size):
    index = np.arange(size)
    angle = (index[:, None] * index[None, :] % size) * (2.0 * math.pi / size)
    cosine = np.cos(angle).astype(ml_dtypes.bfloat16).astype(np.float64)
    sine = np.sin(angle).astype(ml_dtypes.bfloat16).astype(np.float64)
    offset = index[:, None] - index[None, :]
    weight = np.exp(-offset * offset / (2.0 * SIGMA * SIGMA))
    gauss = weight / weight.sum(axis=1, keepdims=True)
    half = size // 2
    columns = np.concatenate([cosine, -sine], axis=1)
    pad = np.zeros((EXTRA - 1, 2 * size))
    real = np.concatenate([cosine, sine], axis=1) / size
    imag = np.concatenate([-sine, cosine], axis=1) / size
    rows = np.concatenate([real[:half], imag[:half], real[half : half + 1], pad, imag[half : half + 1], pad], axis=0)
    back = np.block([[cosine, sine], [-sine, cosine]])
    twice = np.full((1, half), 2.0)
    twice[0, 0] = 1.0
    sines = -sine[:, :half] * twice
    sines[:, 0] = cosine[:, half]
    last = np.concatenate([cosine[:, :half] * twice, sines], axis=1) / size
    wide = np.concatenate([gauss.T, gauss], axis=1)
    narrow = np.concatenate([last, np.zeros((size, size))], axis=1)
    forward = np.concatenate([wide, columns, rows], axis=0)
    backward = np.concatenate([back, narrow], axis=0)
    return jnp.asarray(forward.astype(ml_dtypes.bfloat16)), jnp.asarray(backward.astype(ml_dtypes.bfloat16))


def product(left, right):
    return jnp.dot(left, right, preferred_element_type=jnp.float32)


def spectra_of(panels, table):
    count, size, _ = panels.shape
    right = table[:size, :size]
    if count > 2:
        first = [product(panels[k], right).astype(jnp.bfloat16) for k in range(count)]
    else:
        stack = product(panels.reshape(count * size, size), right).astype(jnp.bfloat16)
        first = [stack[k * size : (k + 1) * size] for k in range(count)]
    gauss = table[:size, size:]
    smooth = [product(gauss, one).astype(jnp.bfloat16) for one in first]
    if count > 2:
        parts = [product(one, table[size : 2 * size]).astype(jnp.bfloat16) for one in smooth]
    else:
        stack = product(jnp.concatenate(smooth, axis=0), table[size : 2 * size]).astype(jnp.bfloat16)
        parts = [stack[k * size : (k + 1) * size] for k in range(count)]
    rows = table[2 * size :]
    return [product(rows, jnp.concatenate([one[:, :size], one[:, size:]], axis=0)) for one in parts]


def spectra_kernel(core, *refs):
    panels, (table, out) = refs[:-2], refs[-2:]

    def work():
        for k, slab in enumerate(spectra_of(jnp.concatenate([p[...] for p in panels], axis=0), table)):
            out[k] = slab

    if core is None:
        work()
    else:
        pl.when(lax.axis_index("chan") == core)(work)


def split(slab, half):
    return (slab[:half], slab[half : 2 * half], slab[2 * half : 2 * half + EXTRA], slab[2 * half + EXTRA :])


def distances(here, chan):
    place = here % PLANE
    one = jnp.where(place % 2 == 0, 1, -1)
    two = jnp.where(place < 2, 2, -2)
    even = chan == 0
    never = 2 * PLANE
    return (
        0,
        jnp.where(even, two, one),
        jnp.where(even, one, two),
        jnp.where(even, -two, never),
        jnp.where(even, never, -two),
        -one,
    )


def cross_slab(a_slab, b_slab, half):
    a_real, a_imag, a_real_x, a_imag_x = split(a_slab, half)
    b_real, b_imag, b_real_x, b_imag_x = split(b_slab, half)
    parts = [
        a_real * b_real + a_imag * b_imag,
        a_imag * b_real - a_real * b_imag,
        a_real_x * b_real_x + a_imag_x * b_imag_x,
        a_imag_x * b_real_x - a_real_x * b_imag_x,
    ]
    return jnp.concatenate(parts, axis=0).astype(jnp.bfloat16)


def write_crosses(first_pair, cuts, ends, blocks, out):
    here = lax.axis_index("tile")
    held = distances(here, lax.axis_index("chan"))
    own = blocks[0]
    tile_dev = own.shape[0]
    half = out.shape[-1] // 2

    for k in range(out.shape[0]):
        pair = first_pair + k
        tile = ends[1, pair]
        away = tile // tile_dev - here
        slot = tile % tile_dev
        mine = ends[0, pair] - here * tile_dev
        for (index, base), source in zip(cuts, blocks):
            size = source.shape[0]
            pick = away == held[index]
            if size < tile_dev:
                pick = pick & (slot >= base) & (slot < base + size)

            @pl.when(pick)
            def _(source=source, base=base):
                out[k] = cross_slab(own[mine], source[slot - base], half)


def cross_other_kernel(cuts, ends, *refs):
    blocks, (panels, table, out, slabs, numbers, sem) = refs[: len(cuts) - 1], refs[len(cuts) - 1 :]
    copy = pltpu.make_async_copy(ends, numbers, sem)
    copy.start()
    for k, slab in enumerate(spectra_of(panels[...], table)):
        slabs[k] = slab
    copy.wait()
    first_pair = out.shape[0] * (1 - lax.axis_index("chan"))
    write_crosses(first_pair, cuts, numbers, (*blocks, slabs), out)


def cross_mine_kernel(cuts, ends, *refs):
    blocks, out = refs[: len(cuts)], refs[len(cuts)]
    write_crosses(out.shape[0] * lax.axis_index("chan"), cuts, ends, blocks, out)


def quotient(slab, half):
    real, imag, real_x, imag_x = split(slab, half)
    magnitude = jnp.sqrt(real * real + imag * imag)
    magnitude_x = jnp.sqrt(real_x * real_x + imag_x * imag_x)
    columns = 2.0 * jnp.sum(magnitude, axis=0, keepdims=True) - magnitude[:1]
    columns = columns + jnp.sum(magnitude_x, axis=0, keepdims=True)
    level = jnp.sum(columns, axis=1, keepdims=True) / (4 * half * half) + 1e-06
    scale = 1.0 / (magnitude + FLOOR * level)
    scale_x = 1.0 / (magnitude_x + FLOOR * level)
    q_real = jnp.concatenate([real * scale, real_x * scale_x], axis=0)
    q_imag = jnp.concatenate([imag * scale, imag_x * scale_x], axis=0)
    return jnp.concatenate([q_real, q_imag], axis=1)


def surface_kernel(spots, mine, other, table, surface, scores, corr, rounded, found, peaks, sem, sems):
    fetch = pltpu.make_async_copy(spots, peaks, sem)
    fetch.start()
    count, _, size = surface.shape
    cand = scores.shape[1]
    half = size // 2
    parts = [quotient(mine[k].astype(jnp.float32) + other[k].astype(jnp.float32), half) for k in range(count)]
    spread = half + EXTRA
    y_all = product(jnp.concatenate(parts, axis=0).astype(jnp.bfloat16), table[: 2 * size])
    last = table[2 * size :, :size]
    copies = []
    for k in range(count):
        y = y_all[k * spread : (k + 1) * spread]
        y_real = y[:half, :size]
        y_imag = y[:half, size:]
        row = lax.broadcasted_iota(jnp.int32, y_imag.shape, 0)
        y_imag = jnp.where(row == 0, y[half : half + 1, :size], y_imag)
        both = jnp.concatenate([y_real, y_imag], axis=0).astype(jnp.bfloat16)
        result = product(last, both)
        corr[k] = result
        rounded[k] = result.astype(jnp.bfloat16)
        copies.append(pltpu.make_async_copy(rounded.at[k], surface.at[k], sems.at[k]))
        copies[-1].start()
    fetch.wait()
    lane = lax.broadcasted_iota(jnp.int32, (1, size), 1)
    diagonal = lax.broadcasted_iota(jnp.int32, (cand, cand), 0) == lax.broadcasted_iota(jnp.int32, (cand, cand), 1)
    for k in range(count):
        picked = []
        for j in range(cand):
            row = corr[k, pl.ds(peaks[k, 0, j], 1), :]
            picked.append(jnp.where(lane == peaks[k, 1, j], row, 0.0))
        sums = jnp.sum(jnp.concatenate(picked, axis=0), axis=1, keepdims=True)
        found[k : k + 1, :] = jnp.sum(jnp.where(diagonal, sums, 0.0), axis=0, keepdims=True)
    copies.append(pltpu.make_async_copy(found, scores, sems.at[count]))
    copies[-1].start()
    for copy in copies:
        copy.wait()


def choose_kernel(first, second, out):
    place = lax.axis_index("tile") % PLANE
    outer = (place == 0) | (place == PLANE - 1)

    @pl.when(outer)
    def _():
        out[...] = first[...]

    @pl.when(jnp.logical_not(outer))
    def _():
        out[...] = second[...]


def routes(devices):
    def up(t, c):
        return (t + PLANE, c) if t + PLANE < devices else (t, 1 - c)

    def down(t, c):
        return (t - PLANE, c) if t >= PLANE else (t, 1 - c)

    def across(c, core):
        return 2 if c == core else 1

    def pairs(step):
        return [(2 * t + c, 2 * d + e) for t in range(devices) for c in range(2) for d, e in [step(t, c)]]

    return (
        pairs(lambda t, c: (t ^ across(c, 0), c)),
        pairs(lambda t, c: (t ^ across(c, 1), c)),
        pairs(lambda t, c: (up if (t % PLANE < 2) == (c == 0) else down)(t, c)),
        pairs(lambda t, c: (t ^ across(c, 1), c)),
        pairs(lambda t, c: (up if (t % PLANE < 2) == (c == 1) else down)(t, c)),
    )


def after(value, *earlier):
    return lax.optimization_barrier((value, *earlier))[0]


def call(kernel, name, operands, out, scratch=(), first=VMEM, flops=1 << 30, results=VMEM):
    return pl.pallas_call(
        kernel,
        out_shape=out,
        in_specs=[first] + [VMEM] * (len(operands) - 1),
        out_specs=jax.tree.map(lambda _: results, out),
        scratch_shapes=scratch,
        compiler_params=pltpu.CompilerParams(vmem_limit_bytes=8 << 20),
        cost_estimate=pl.CostEstimate(flops=flops, bytes_accessed=1 << 20, transcendentals=0),
        name=name,
    )(*operands)


def spectra_calls(table, slab, name, core, *panels, flops=None):
    count, size = sum(p.shape[0] for p in panels), panels[0].shape[-1]
    return call(
        functools.partial(spectra_kernel, core),
        "spectra_" + name,
        (*panels, table),
        jax.ShapeDtypeStruct((count, slab, size), jnp.float32),
        flops=flops or count * 12 * size**3,
    )


def chosen(first, second, flops):
    return call(choose_kernel, "choose", (first, second), jax.ShapeDtypeStruct(first.shape, first.dtype), flops=flops)


def shards(panels, pair_ends, peaks):
    tile_dev, _, size, _ = panels.shape
    share, cand, _ = peaks.shape
    devices = lax.axis_size("tile")
    local = panels[:, 0]
    forward, backward = tables(size)
    slab = size + 2 * EXTRA
    swap, cross_swap, climb, relay, climb_late = routes(devices)
    move = functools.partial(lax.ppermute, axis_name=BOTH)
    ends = pair_ends.T
    spots = jnp.transpose(peaks, (0, 2, 1))
    half = tile_dev // 2

    spectra = functools.partial(spectra_calls, forward, slab)
    parts = (local[:half], lax.optimization_barrier(local)[half:])
    got_swap = [move(part, perm=swap) for part in parts]
    own = spectra("own", None, *parts)
    got_cross = [move(after(part, got_swap[0], own), perm=cross_swap) for part in parts]
    got_climb = [move(part, perm=climb) for part in got_swap]
    picked = [chosen(a, b, flops) for a, b, flops in zip(got_swap, got_climb, (1 << 20, 3_000_000_000))]
    got_relay = [move(part, perm=relay) for part in picked]
    got_late = [move(part, perm=climb_late) for part in got_cross]
    from_swap = spectra("swap", None, after(got_swap[0], got_relay[0]), got_swap[1])
    from_cross = spectra("cross", None, *got_cross, flops=1_000_000)
    from_climb = spectra("climb", 0, after(got_climb[0], from_swap), got_climb[1], flops=1_000_000)
    from_relay = spectra("relay", None, got_relay[0], flops=800_000_000)
    from_late = spectra("late", 1, *got_late)
    blocks = [own, from_swap, from_cross, from_climb, from_late, from_relay]
    cuts = [(index, 0) for index in range(len(blocks))] + [(len(blocks) - 1, half)]
    crosses = jax.ShapeDtypeStruct((share, slab, size), jnp.bfloat16)
    given, last = call(
        functools.partial(cross_other_kernel, cuts),
        "cross_other",
        (ends, *blocks, got_relay[1], forward),
        (crosses, jax.ShapeDtypeStruct((tile_dev - half, slab, size), jnp.float32)),
        [pltpu.SMEM(ends.shape, ends.dtype), pltpu.SemaphoreType.DMA(())],
        ANY,
        flops=1 << 29,
    )
    other = lax.ppermute(given, "chan", [(0, 1), (1, 0)])
    kept = call(
        functools.partial(cross_mine_kernel, cuts),
        "cross_mine",
        (ends, *blocks, last),
        crosses,
        first=SMEM,
        flops=1 << 25,
    )
    return call(
        surface_kernel,
        "surface",
        (spots, kept, other, backward),
        (jax.ShapeDtypeStruct((share, size, size), jnp.bfloat16), jax.ShapeDtypeStruct((share, cand), jnp.float32)),
        [
            pltpu.VMEM((share, size, size), jnp.float32),
            pltpu.VMEM((share, size, size), jnp.bfloat16),
            pltpu.VMEM((share, cand), jnp.float32),
            pltpu.SMEM(spots.shape, spots.dtype),
            pltpu.SemaphoreType.DMA(()),
            pltpu.SemaphoreType.DMA((share + 1,)),
        ],
        ANY,
        results=ANY,
    )


def solution(mesh):
    in_specs = (P("tile", "chan", None, None), P("tile", None), P(BOTH, None, None))
    out_specs = (P(BOTH, None, None), P(BOTH, None))
    return jax.shard_map(shards, mesh=mesh, in_specs=in_specs, out_specs=out_specs, check_vma=False)
```
